1024 devices in a mesh: dom: 16 (over x, core), grp: 64 (over y, z).
Axes of the slice: x: 8, y: 8, z: 8, core: 2. Of those that a mesh axis runs over, the one named last changes fastest.
Arguments:
- features: bfloat16 [16, 32768, 256], P('dom', 'grp'), may hold values from -6 to 6
- send_list: int32 [16, 64, 16, 2], P('dom', 'grp'), may hold values from -1 to 3, as said below
- nbr_count: int32 [16, 64, 4], P('dom', 'grp'), may hold values from 9 to 12, as said below
- nbr_index: int32 [16, 64, 4, 12], P('dom', 'grp'), may hold values from 0 to 37, as said below
- tiles: bfloat16 [16, 256, 12, 128, 128], P('dom', 'grp'), as said below
- degree: int32 [16, 32768], P('dom', 'grp'), may hold values from 1 to 36, as said below
- w_self: bfloat16 [256, 256], replicated, may hold values from -0.375 to 0.375
- w_nbr: bfloat16 [256, 256], replicated, may hold values from -0.375 to 0.375
- bias: float32 [256], replicated, may hold values from -4 to 4
- cotangent: bfloat16 [16, 32768, 256], P('dom', 'grp'), may hold values from -6 to 6
Outputs:
- hidden_out: bfloat16 [16, 32768, 256], P('dom', 'grp')
- feat_grad: float32 [16, 32768, 256], P('dom', 'grp')
- w_self_grad: float32 [256, 256], replicated
- w_nbr_grad: float32 [256, 256], replicated
- bias_grad: float32 [256], replicated
The draws below stay inside these ranges and needn't reach their ends.
Inputs may be any that keep to these rules, and one draw needn't show every extreme that they name: send_list[d, g, p, s] is the local block that the device at dom index d and grp index g sends to dom peer p in slot s, or -1 for an empty slot; for each peer the live slots come first; a device sends nothing to itself; in every slab one device is sent all 2 slots by every other peer, and every device fills all 2 slots for at least one peer. nbr_count[d, g, b] is how many leading entries of block b's source list are live; on every device some block has all 12 live. `nbr_index`: entries past the count are ignored and hold arbitrary table entries; every table entry from 4 on is named by at least one live entry of the device's lists. `tiles`: each row of a tile has at most 3 nonzero entries. degree of a node is the number of nonzero entries of its row in the tiles of its block's live source list, or 1 where there are none.
All inputs are finite; a program needn't handle non-finite values.
Results may differ from the reference program's by a relative error of at most 0.0075.
Values may be sent and summed in bfloat16 or wider, within the bound.
No kernel may reach another device: no remote copies, remote signals or barrier semaphores. Data moves between devices by JAX's collectives and lax.ppermute only.
A program may use at most 64 MiB of HBM per device.

```python
import jax
import jax.numpy as jnp
from jax import lax

F = 256
BLK = 128
NB = 4
KN = 12
SLOTS = 2
NODES = 32768
N_DOM = 16
N_GRP = 64


def adjacency_draw(key):
    key_a, key_b, key_c, key_d, key_e = jax.random.split(key, 5)
    counts = jax.random.randint(key_a, (N_DOM, N_GRP, NB), KN - KN // 4, KN + 1)
    full_block = jax.random.randint(key_b, (N_DOM, N_GRP, 1), 0, NB)
    counts = jnp.where(jnp.arange(NB)[None, None, :] == full_block, KN, counts).astype(jnp.int32)
    link_ids = jnp.arange(KN, dtype=jnp.int32)
    live_links = link_ids[None, None, None, :] < counts[..., None]
    below = jnp.sum(jnp.minimum(counts[..., :, None], link_ids), axis=-2)
    ahead = (counts[..., :, None] > link_ids).astype(jnp.int32)
    link_rank = below[..., None, :] + jnp.cumsum(ahead, axis=-2) - ahead
    needed = N_DOM * SLOTS + 2
    sub_keys = jax.random.split(key_c, N_DOM * N_GRP)
    orders = jax.vmap(lambda sub_key: jax.random.permutation(sub_key, needed))(sub_keys)
    orders = orders.reshape(N_DOM, N_GRP, needed).astype(jnp.int32)
    flat_rank = jnp.clip(link_rank, 0, needed - 1).reshape(N_DOM, N_GRP, NB * KN)
    picked = jnp.take_along_axis(orders, flat_rank, axis=-1).reshape(N_DOM, N_GRP, NB, KN)
    local_ids = jax.random.randint(key_d, (N_DOM, N_GRP, NB, KN), 0, NB)
    spare_ids = jax.random.randint(key_e, (N_DOM, N_GRP, NB, KN), 0, NB + needed)
    sources = jnp.where(live_links, jnp.where(link_rank < needed, NB + picked, local_ids), spare_ids)
    return (counts, sources.astype(jnp.int32))


def tile_pattern(key):
    counts, sources = adjacency_draw(jax.random.fold_in(key, 7))
    own_key = jax.random.fold_in(key, 13)
    key_a, key_b, key_c = jax.random.split(own_key, 3)
    shape = (N_DOM, N_GRP * NB, KN, BLK)
    per_row = jax.random.randint(key_a, shape, 0, 4)
    full_at = jnp.argmax(counts[0, 0] == KN).astype(jnp.int32)
    dom_ids = jnp.arange(N_DOM, dtype=jnp.int32)[:, None, None, None]
    block_ids = jnp.arange(N_GRP * NB, dtype=jnp.int32)[None, :, None, None]
    row_ids = jnp.arange(BLK, dtype=jnp.int32)[None, None, None, :]
    at_full = (dom_ids == 0) & (block_ids == full_at)
    per_row = jnp.where(at_full & (row_ids == 0), 3, jnp.where(at_full & (row_ids == 1), 0, per_row))
    stride = 2 * jax.random.randint(key_b, shape, 0, BLK // 2) + 1
    offset = jax.random.randint(key_c, shape, 0, BLK)
    return (per_row.astype(jnp.int32), stride.astype(jnp.int32), offset.astype(jnp.int32), counts)


def draw_tiles(key, part):
    per_row, stride, offset, counts = tile_pattern(key)
    key = jax.random.fold_in(key, 17)
    columns = jnp.arange(BLK, dtype=jnp.int32)
    placed = (columns * stride[..., None] + offset[..., None]) % BLK
    mask = placed < per_row[..., None]
    values = jax.random.uniform(key, mask.shape, jnp.float32, 0.5, 1.5)
    return jnp.where(mask, values, 0.0).astype(jnp.bfloat16)


def draw_degree(key, part):
    per_row, stride, offset, counts = tile_pattern(key)
    live = jnp.arange(KN, dtype=jnp.int32)[None, None, None, :] < counts[..., None]
    grid = per_row.reshape(N_DOM, N_GRP, NB, KN, BLK)
    total = jnp.sum(jnp.where(live[..., None], grid, 0), axis=3)
    return jnp.maximum(total, 1).reshape(N_DOM, N_GRP * NB * BLK).astype(jnp.int32)


def draw_nbr_count(key, part):
    counts, sources = adjacency_draw(jax.random.fold_in(key, 7))
    return counts


def draw_nbr_index(key, part):
    counts, sources = adjacency_draw(jax.random.fold_in(key, 7))
    return sources


def draw_send_list(key, part):
    key = jax.random.fold_in(key, 11)
    key_a, key_b, key_c, key_d = jax.random.split(key, 4)
    holder = jnp.arange(N_DOM).reshape(N_DOM, 1, 1)
    peer_ids = jnp.arange(N_DOM).reshape(1, 1, N_DOM)
    counts = jax.random.randint(key_a, (N_DOM, N_GRP, N_DOM), 0, SLOTS + 1)
    offset = jax.random.randint(key_b, (N_DOM, N_GRP, 1), 1, max(N_DOM, 2))
    favored = (holder + offset) % N_DOM
    target = jax.random.randint(key_c, (1, N_GRP, 1), 0, N_DOM)
    counts = jnp.where((peer_ids == favored) | (peer_ids == target), SLOTS, counts)
    counts = jnp.where(peer_ids == holder, 0, counts)
    slot_ids = jnp.arange(SLOTS).reshape(1, 1, 1, SLOTS)
    blocks = jax.random.randint(key_d, (N_DOM, N_GRP, N_DOM, SLOTS), 0, NB)
    return jnp.where(slot_ids < counts[..., None], blocks, -1).astype(jnp.int32)


def steps_of(stream_key, dims, shards, low, top_value):
    def one(dim, blocks):
        draws = jax.random.uniform(jax.random.fold_in(jax.random.fold_in(stream_key, 6), dim), (blocks,), jnp.float32, low / len(shards), top_value / len(shards))
        return jnp.repeat(jnp.exp(draws), dims[dim] // blocks).reshape((-1,) + (1,) * (len(dims) - dim - 1))

    gain = one(*shards[0])
    for cut in shards[1:]:
        gain = gain * one(*cut)
    return gain


def bell_draw(stream_key, shape, width, bound, cuts=(), kind=jnp.bfloat16):
    level = steps_of(stream_key, shape, cuts, -0.22, 0.18) if cuts else 1.0
    array = jax.random.normal(stream_key, shape, jnp.float32) * width * level
    return jnp.minimum(jnp.maximum(array, -bound), bound).astype(kind)


def setup_inputs(seed: int = 0) -> dict:
    arg_keys = jax.random.split(jax.random.key(seed), 11)
    features = bell_draw(arg_keys[0], (N_DOM, NODES, F), 1.0, 6.0, ((0, 16), (1, 64)))
    send_list = draw_send_list(jax.random.fold_in(arg_keys[10], 71), 0)
    nbr_count = draw_nbr_count(jax.random.fold_in(arg_keys[10], 71), 0)
    nbr_index = draw_nbr_index(jax.random.fold_in(arg_keys[10], 71), 0)
    tiles = draw_tiles(jax.random.fold_in(arg_keys[10], 71), 0)
    degree = draw_degree(jax.random.fold_in(arg_keys[10], 71), 0)
    w_self = bell_draw(arg_keys[6], (F, F), F ** -0.5, 0.375)
    w_nbr = bell_draw(arg_keys[7], (F, F), F ** -0.5, 0.375)
    bias = bell_draw(arg_keys[8], (F,), 1.0, 4.0, (), jnp.float32)
    cotangent = bell_draw(arg_keys[9], (N_DOM, NODES, F), 1.0, 6.0, ((0, 16), (1, 64)))
    return {"features": features, "send_list": send_list, "nbr_count": nbr_count, "nbr_index": nbr_index, "tiles": tiles, "degree": degree, "w_self": w_self, "w_nbr": w_nbr, "bias": bias, "cotangent": cotangent}


def reference(features, send_list, nbr_count, nbr_index, tiles, degree, w_self, w_nbr, bias, cotangent):
    blocked = features.reshape(N_DOM, N_GRP, NB, BLK, F)
    tile_grid = tiles.reshape(N_DOM, N_GRP, NB, KN, BLK, BLK)
    spread = degree.reshape(N_DOM, N_GRP, NB * BLK).astype(jnp.float32)
    upstream = cotangent.reshape(N_DOM, N_GRP, NB * BLK, F)
    table_size = NB + 2 + N_DOM * SLOTS
    peer_ids = jnp.arange(N_DOM, dtype=jnp.int32)[:, None]
    link_ids = jnp.arange(KN, dtype=jnp.int32)[None, :]
    zero_block = jnp.zeros((BLK, F), jnp.bfloat16)

    def one_device(totals, position):
        grad_acc, grad_self, grad_nbr, grad_bias = totals
        dom_at = position // N_GRP
        grp_at = position % N_GRP
        below_at = jnp.maximum(grp_at - 1, 0).astype(jnp.int32)
        above_at = jnp.minimum(grp_at + 1, N_GRP - 1).astype(jnp.int32)
        has_below = grp_at > 0
        has_above = grp_at < N_GRP - 1
        own_rows = blocked[dom_at, grp_at]
        below_rim = jnp.where(has_below, blocked[dom_at, below_at, NB - 1], zero_block)
        above_rim = jnp.where(has_above, blocked[dom_at, above_at, 0], zero_block)
        sent_ids = send_list[:, grp_at, dom_at, :]
        filled = (sent_ids >= 0)[:, :, None, None]
        safe_ids = jnp.maximum(sent_ids, 0).astype(jnp.int32)
        arrived = jnp.where(filled, blocked[peer_ids, grp_at, safe_ids], jnp.zeros((), jnp.bfloat16))
        source_table = jnp.concatenate([own_rows, below_rim[None], above_rim[None], arrived.reshape(N_DOM * SLOTS, BLK, F)], axis=0)
        sources = nbr_index[dom_at, grp_at]
        live_links = link_ids < nbr_count[dom_at, grp_at][:, None]
        weights = jnp.where(live_links[:, :, None, None], tile_grid[dom_at, grp_at], jnp.zeros((), jnp.bfloat16))
        picked = source_table[sources]
        summed = jnp.einsum('bkij,bkjf->bif', weights.astype(jnp.float32), picked.astype(jnp.float32))
        rows_deg = spread[dom_at, grp_at][:, None]
        mean_rows = (summed.reshape(NB * BLK, F) / rows_deg).astype(jnp.bfloat16)
        flat_rows = own_rows.reshape(NB * BLK, F)
        pre_act = jnp.dot(flat_rows, w_self, preferred_element_type=jnp.float32) + jnp.dot(mean_rows, w_nbr, preferred_element_type=jnp.float32) + bias
        hidden = jax.nn.silu(pre_act).astype(jnp.bfloat16)
        gate_sig = jax.nn.sigmoid(pre_act)
        silu_slope = gate_sig * (1.0 + pre_act * (1.0 - gate_sig))
        pre_grad = (upstream[dom_at, grp_at].astype(jnp.float32) * silu_slope).astype(jnp.bfloat16)
        grad_self = grad_self + jnp.dot(flat_rows.T, pre_grad, preferred_element_type=jnp.float32)
        grad_nbr = grad_nbr + jnp.dot(mean_rows.T, pre_grad, preferred_element_type=jnp.float32)
        grad_bias = grad_bias + lax.optimization_barrier(jnp.sum(pre_grad.astype(jnp.float32), axis=0))
        self_grad = jnp.dot(pre_grad, w_self.T, preferred_element_type=jnp.float32)
        mean_grad = jnp.dot(pre_grad, w_nbr.T, preferred_element_type=jnp.float32)
        sum_grad = (mean_grad / rows_deg).astype(jnp.bfloat16).reshape(NB, BLK, F)
        link_grad = jnp.einsum('bkij,bif->bkjf', weights.astype(jnp.float32), sum_grad.astype(jnp.float32))
        table_grad = jnp.zeros((table_size, BLK, F), jnp.float32).at[sources.reshape(NB * KN)].add(link_grad.reshape(NB * KN, BLK, F))
        rounded = lax.optimization_barrier(table_grad[NB:].astype(jnp.bfloat16)).astype(jnp.float32)
        grad_acc = grad_acc.at[dom_at, grp_at].add(self_grad.reshape(NB, BLK, F) + table_grad[:NB])
        grad_acc = grad_acc.at[dom_at, below_at, NB - 1].add(jnp.where(has_below, rounded[0], 0.0))
        grad_acc = grad_acc.at[dom_at, above_at, 0].add(jnp.where(has_above, rounded[1], 0.0))
        returned = jnp.where(filled, rounded[2:].reshape(N_DOM, SLOTS, BLK, F), 0.0)
        grad_acc = grad_acc.at[peer_ids, grp_at, safe_ids].add(returned)
        return ((grad_acc, grad_self, grad_nbr, grad_bias), hidden)
    start = (jnp.zeros((N_DOM, N_GRP, NB, BLK, F), jnp.float32), jnp.zeros((F, F), jnp.float32), jnp.zeros((F, F), jnp.float32), jnp.zeros((F,), jnp.float32))
    finals, hiddens = lax.scan(one_device, start, jnp.arange(N_DOM * N_GRP, dtype=jnp.int32))
    grad_acc, grad_self, grad_nbr, grad_bias = finals
    factor = 1.0 / jnp.sqrt(jnp.float32(N_DOM * NODES))
    hidden_out = hiddens.reshape(N_DOM, NODES, F)
    feat_grad = grad_acc.reshape(N_DOM, NODES, F)
    return (hidden_out, feat_grad, grad_self * factor, grad_nbr * factor, grad_bias * factor)
```

```python
import functools
import math

import jax
import jax.numpy as jnp
from jax import lax
from jax.experimental import pallas as pl
from jax.experimental.pallas import tpu as pltpu
from jax.sharding import PartitionSpec as P

BLK = 128
F32 = jnp.float32
BF16 = jnp.bfloat16
ROWS_T = (((0,), (0,)), ((), ()))
COLS_T = (((1,), (1,)), ((), ()))


def dot(a, b, dims=(((1,), (0,)), ((), ()))):
    return lax.dot_general(a, b, dims, preferred_element_type=F32)


def block(t):
    return pl.ds(pl.multiple_of(t * BLK, BLK), BLK)


def layer_kernel(
    blocks_n,
    links_n,
    slots_n,
    recv_ref,
    count_ref,
    index_ref,
    gathered_ref,
    below_ref,
    above_ref,
    rows_ref,
    tiles_ref,
    degree_ref,
    w_self_ref,
    w_nbr_ref,
    bias_ref,
    cot_ref,
    hidden_ref,
    base_ref,
    rims_ref,
    sends_ref,
    weights_ref,
    table,
    grads,
    sems,
):
    rows_n, width = rows_ref.shape
    halo = blocks_n + 2
    table_n = halo + slots_n
    copies = [
        pltpu.make_async_copy(below_ref, table.at[pl.ds(blocks_n * BLK, BLK)], sems.at[0]),
        pltpu.make_async_copy(above_ref, table.at[pl.ds((blocks_n + 1) * BLK, BLK)], sems.at[1]),
    ]
    peers_n, per_peer = recv_ref.shape
    for slot in range(slots_n):
        peer = slot // per_peer
        source = peer * blocks_n + jnp.maximum(recv_ref[peer, slot % per_peer], 0)
        copies.append(
            pltpu.make_async_copy(
                gathered_ref.at[block(source)],
                table.at[pl.ds((halo + slot) * BLK, BLK)],
                sems.at[2 + slot],
            )
        )
    for copy in copies:
        copy.start()

    rows = rows_ref[...]
    table[pl.ds(0, rows_n)] = rows
    table[pl.ds(table_n * BLK, BLK)] = jnp.zeros((BLK, width), BF16)
    grads[...] = jnp.zeros_like(grads)
    self_act = dot(rows, w_self_ref[...])
    spreads = []
    for b in range(blocks_n):
        line = degree_ref[pl.ds(b, 1), :].astype(F32)
        column = jnp.transpose(jnp.broadcast_to(line, (BLK, BLK)))
        spreads.append(jnp.concatenate([column] * (width // BLK), axis=1))
    entries = []
    owners = []
    for b in range(blocks_n):
        for k in range(links_n):
            entry = index_ref[b, k]
            slot = jnp.maximum(entry - halo, 0)
            peer = slot // per_peer
            owner = recv_ref[peer, slot % per_peer]
            is_slot = entry >= halo
            dead = (k >= count_ref[b]) | (is_slot & (owner < 0))
            entries.append(jnp.where(dead, table_n, entry))
            owner = jnp.where(is_slot, halo + peer * blocks_n + owner, entry)
            owners.append(jnp.where(dead, halo + peers_n * blocks_n, owner))

    for copy in copies:
        copy.wait()

    means = []
    for b in range(blocks_n):
        total = None
        for k in range(0, links_n, 2):
            at = b * links_n + k
            left = jnp.concatenate([tiles_ref[at], tiles_ref[at + 1]], axis=1)
            right = jnp.concatenate([table[block(entries[at])], table[block(entries[at + 1])]], axis=0)
            term = dot(left, right)
            total = term if total is None else total + term
        means.append((total / spreads[b]).astype(BF16))
    mean_rows = jnp.concatenate(means, axis=0)
    pre_act = self_act + dot(mean_rows, w_nbr_ref[...]) + bias_ref[...]
    gate = jax.nn.sigmoid(pre_act)
    hidden_ref[...] = (pre_act * gate).astype(BF16)
    slope = gate * (1.0 + pre_act * (1.0 - gate))
    pre_grad = (cot_ref[...].astype(F32) * slope).astype(BF16)
    parts, each = weights_ref.shape[:2]
    grad_self = dot(rows, pre_grad, ROWS_T)
    grad_nbr = dot(mean_rows, pre_grad, ROWS_T)
    half = parts // 2
    weights_ref[pl.ds(0, half), :, pl.ds(0, width)] = grad_self.reshape(half, each, width)
    weights_ref[pl.ds(half, half), :, pl.ds(0, width)] = grad_nbr.reshape(half, each, width)
    bias_sum = jnp.sum(pre_grad.astype(F32), axis=0, keepdims=True)
    lines = [bias_sum[:, i * BLK : (i + 1) * BLK] for i in range(width // BLK)]
    lines.append(jnp.zeros((each - len(lines), BLK), F32))
    bias_tile = jnp.concatenate(lines, axis=0)
    weights_ref[:, :, pl.ds(width, BLK)] = jnp.broadcast_to(bias_tile[None], (parts, each, BLK))

    mean_grad = dot(pre_grad, w_nbr_ref[...], COLS_T)
    for b in range(blocks_n):
        sum_grad = (mean_grad[b * BLK : (b + 1) * BLK] / spreads[b]).astype(BF16)
        for k in range(links_n):
            at = b * links_n + k
            where = block(owners[at])
            grads[where] += dot(tiles_ref[at], sum_grad, ROWS_T)
    base_ref[...] = dot(pre_grad, w_self_ref[...], COLS_T) + grads[pl.ds(0, rows_n)]
    rims_ref[...] = grads[pl.ds(rows_n, 2 * BLK)].astype(BF16)
    for p in range(peers_n):
        sends_ref[pl.ds(p * rows_n, rows_n)] = grads[pl.ds(halo * BLK + p * rows_n, rows_n)].astype(BF16)


def layer(recv, count, index, gathered, below, above, rows, tiles, degree, w_self, w_nbr, bias, cot, parts):
    blocks_n, links_n = index.shape
    slots_n = recv.size
    rows_n, width = rows.shape
    table_n = blocks_n + 2 + slots_n
    owners_n = blocks_n + 2 + recv.shape[0] * blocks_n
    smem = pl.BlockSpec(memory_space=pltpu.SMEM)
    hbm = pl.BlockSpec(memory_space=pl.ANY)
    vmem = pl.BlockSpec(memory_space=pltpu.VMEM)
    each = 2 * width // parts
    return pl.pallas_call(
        functools.partial(layer_kernel, blocks_n, links_n, slots_n),
        out_shape=(
            jax.ShapeDtypeStruct((rows_n, width), BF16),
            jax.ShapeDtypeStruct((rows_n, width), F32),
            jax.ShapeDtypeStruct((2 * BLK, width), BF16),
            jax.ShapeDtypeStruct((recv.shape[0] * rows_n, width), BF16),
            jax.ShapeDtypeStruct((parts, each, width + BLK), F32),
        ),
        in_specs=[smem] * 3 + [hbm] * 3 + [vmem] * 7,
        out_specs=(vmem,) * 5,
        scratch_shapes=[
            pltpu.VMEM(((table_n + 1) * BLK, width), BF16),
            pltpu.VMEM(((owners_n + 1) * BLK, width), F32),
            pltpu.SemaphoreType.DMA((2 + slots_n,)),
        ],
        compiler_params=pltpu.CompilerParams(vmem_limit_bytes=48 * 2**20),
        cost_estimate=pl.CostEstimate(
            flops=1_300_000_000, bytes_accessed=12_000_000, transcendentals=rows_n * width
        ),
        name="layer",
    )(recv, count, index, gathered, below, above, rows, tiles, degree, w_self, w_nbr, bias, cot)


def shift(block_rows, axis, step):
    count = lax.axis_size(axis)
    pairs = [(i, i + step) for i in range(count) if 0 <= i + step < count]
    return lax.ppermute(block_rows, axis, pairs)


def swap(array, axis):
    return lax.all_to_all(array, axis, split_axis=0, concat_axis=0, tiled=True)


def on_device(
    features, send_list, nbr_count, nbr_index, tiles, degree, w_self, w_nbr, bias, cotangent
):
    rows = features[0]
    rows_n, width = rows.shape
    blocks_n = rows_n // BLK
    links_n = nbr_index.shape[-1]
    groups = lax.axis_size("grp")
    doms = lax.axis_size("dom")

    with jax.named_scope("gather_rows"):
        gathered = lax.all_gather(rows, "dom", tiled=True)
    with jax.named_scope("send_lists"):
        recv = swap(send_list[0, 0], "dom")
    with jax.named_scope("rims"):
        below = shift(rows[rows_n - BLK :], "grp", 1)
        above = shift(rows[:BLK], "grp", -1)

    hidden, base, rims, sends, partial = layer(
        recv,
        nbr_count[0, 0],
        nbr_index[0, 0],
        gathered,
        below,
        above,
        rows,
        tiles.reshape(blocks_n * links_n, BLK, BLK),
        degree.reshape(blocks_n, BLK),
        w_self,
        w_nbr,
        bias.reshape(1, width),
        cotangent[0],
        groups,
    )

    with jax.named_scope("return_slots"):
        returned = lax.psum_scatter(sends, "dom", tiled=True)
    with jax.named_scope("return_rims"):
        from_above = shift(rims[:BLK], "grp", -1)
        from_below = shift(rims[BLK:], "grp", 1)
    with jax.named_scope("weight_sums"):
        chunk = jnp.sum(swap(partial, "grp"), axis=0)
        chunk = jnp.sum(lax.all_gather(chunk, "dom"), axis=0)
        chunk = chunk * (1.0 / math.sqrt(rows_n * doms * groups))
        bias_grad = chunk[: width // BLK, width:].reshape(width)
        whole = swap(jnp.broadcast_to(chunk[None, :, :width], (groups,) + chunk[:, :width].shape), "grp")
        whole = whole.reshape(2 * width, width)
    edges = jnp.concatenate(
        [from_below, jnp.zeros((rows_n - 2 * BLK, width), BF16), from_above], axis=0
    )
    feat_grad = base + returned.astype(F32) + edges.astype(F32)
    return hidden[None], feat_grad[None], whole[:width], whole[width:], bias_grad


def solution(mesh):
    in_specs = (
        P("dom", "grp", None),
        P("dom", "grp", None, None),
        P("dom", "grp", None),
        P("dom", "grp", None, None),
        P("dom", "grp", None, None, None),
        P("dom", "grp"),
        P(),
        P(),
        P(),
        P("dom", "grp", None),
    )
    out_specs = (P("dom", "grp", None), P("dom", "grp", None), P(), P(), P())
    return jax.shard_map(
        on_device, mesh=mesh, in_specs=in_specs, out_specs=out_specs, check_vma=False
    )
```

```python
import functools
import math

import jax
import jax.numpy as jnp
from jax import lax
from jax.experimental import pallas as pl
from jax.experimental.pallas import tpu as pltpu
from jax.sharding import PartitionSpec as P

BLK = 128
PAD = 16
SCALE = 8192.0
F32 = jnp.float32
BF16 = jnp.bfloat16
ROWS_T = (((0,), (0,)), ((), ()))
COLS_T = (((1,), (1,)), ((), ()))


def dot(a, b, dims=(((1,), (0,)), ((), ()))):
    return lax.dot_general(a, b, dims, preferred_element_type=F32)


def block(t):
    return pl.ds(pl.multiple_of(t * BLK, BLK), BLK)


def layer_kernel(
    blocks_n,
    links_n,
    peers_n,
    per_peer,
    plan_ref,
    gathered_ref,
    below_ref,
    above_ref,
    rows_hbm,
    tiles_hbm,
    degree_hbm,
    w_self_hbm,
    w_nbr_hbm,
    bias_hbm,
    cot_hbm,
    hidden_ref,
    base_ref,
    rims_ref,
    sends_ref,
    weights_ref,
    tiles_ref,
    degree_ref,
    w_self_ref,
    w_nbr_ref,
    bias_ref,
    cot_ref,
    table,
    grads,
    own_sems,
    tile_sems,
    table_sems,
):
    rows_n, width = cot_ref.shape
    halo = blocks_n + 2
    slots_n = peers_n * per_peer
    table_n = halo + slots_n
    rows_ref = table.at[pl.ds(0, rows_n)]
    own = [
        pltpu.make_async_copy(source, target, own_sems.at[i])
        for i, (source, target) in enumerate(
            (
                (rows_hbm, rows_ref),
                (w_self_hbm, w_self_ref),
                (degree_hbm, degree_ref),
                (bias_hbm, bias_ref),
                (w_nbr_hbm, w_nbr_ref),
                (cot_hbm, cot_ref),
            )
        )
    ]
    tile_copies = [
        pltpu.make_async_copy(
            tiles_hbm.at[pl.ds(b * links_n, links_n)],
            tiles_ref.at[pl.ds(b * links_n, links_n)],
            tile_sems.at[b],
        )
        for b in range(blocks_n)
    ]
    table_copies = [
        pltpu.make_async_copy(below_ref, table.at[pl.ds(blocks_n * BLK, BLK)], table_sems.at[0]),
        pltpu.make_async_copy(above_ref, table.at[pl.ds((blocks_n + 1) * BLK, BLK)], table_sems.at[1]),
    ]
    for slot in range(slots_n):
        source = (slot // per_peer) * (rows_n + PAD) + jnp.maximum(plan_ref[slot], 0) * BLK
        table_copies.append(
            pltpu.make_async_copy(
                gathered_ref.at[pl.ds(pl.multiple_of(source, PAD), BLK)],
                table.at[pl.ds((halo + slot) * BLK, BLK)],
                table_sems.at[2 + slot],
            )
        )
    for copy in own + table_copies + tile_copies:
        copy.start()

    table[pl.ds(table_n * BLK, BLK)] = jnp.zeros((BLK, width), BF16)
    grads[...] = jnp.zeros_like(grads)
    entries = []
    owners = []
    for b in range(blocks_n):
        count = plan_ref[slots_n + b]
        for k in range(links_n):
            entry = plan_ref[slots_n + blocks_n + b * links_n + k]
            is_slot = entry >= halo
            slot = jnp.maximum(entry - halo, 0)
            owner = plan_ref[slot]
            dead = (k >= count) | (is_slot & (owner < 0))
            entries.append(jnp.where(dead, table_n, entry))
            owner = jnp.where(is_slot, halo + (slot // per_peer) * blocks_n + owner, entry)
            owners.append(jnp.where(dead, halo + peers_n * blocks_n, owner))

    for copy in own:
        copy.wait()
    rows = rows_ref[...]
    self_act = dot(rows, w_self_ref[...]) + bias_ref[...]
    spreads = []
    for b in range(blocks_n):
        line = degree_ref[pl.ds(b, 1), :].astype(F32)
        column = jnp.transpose(jnp.broadcast_to(line, (BLK, BLK)))
        spreads.append(jnp.concatenate([column] * (width // BLK), axis=1))
    for copy in table_copies:
        copy.wait()

    means = []
    for b in range(blocks_n):
        tile_copies[b].wait()
        total = None
        for k in range(0, links_n, 2):
            at = b * links_n + k
            left = jnp.concatenate([tiles_ref[at], tiles_ref[at + 1]], axis=1)
            right = jnp.concatenate([table[block(entries[at])], table[block(entries[at + 1])]], axis=0)
            term = dot(left, right)
            total = term if total is None else total + term
        means.append((total / spreads[b]).astype(BF16))
    mean_rows = jnp.concatenate(means, axis=0)
    pre_act = self_act + dot(mean_rows, w_nbr_ref[...])
    gate = jax.nn.sigmoid(pre_act)
    hidden_ref[...] = (pre_act * gate).astype(BF16)
    slope = gate * (1.0 + pre_act * (1.0 - gate))
    pre_grad = (cot_ref[...].astype(F32) * slope).astype(BF16)
    grad_all = jnp.concatenate([dot(rows, pre_grad, ROWS_T), dot(mean_rows, pre_grad, ROWS_T)], axis=0)
    grad_all = grad_all.astype(BF16)
    bias_sum = jnp.sum(pre_grad.astype(F32), axis=0, keepdims=True)
    parts, each = weights_ref.shape[0], weights_ref.shape[1] // 2
    halves = width // BLK
    lines = [bias_sum[:, i * BLK : (i + 1) * BLK] for i in range(halves)]
    lines.append(jnp.zeros((each - halves, BLK), F32))
    bias_tile = jnp.concatenate(lines, axis=0).astype(BF16)
    stride = parts // halves
    for i in range(halves):
        chunk = grad_all[:, i * BLK : (i + 1) * BLK].reshape(stride, each, BLK)
        weights_ref[pl.ds(i * stride, stride), pl.ds(0, each), :] = chunk
    weights_ref[:, pl.ds(each, each), :] = jnp.broadcast_to(bias_tile[None], (parts, each, BLK))

    mean_grad = dot(pre_grad, w_nbr_ref[...], COLS_T)
    for b in range(blocks_n):
        sum_grad = (mean_grad[b * BLK : (b + 1) * BLK] / spreads[b]).astype(BF16)
        for k in range(links_n):
            at = b * links_n + k
            where = block(owners[at])
            grads[where] += dot(tiles_ref[at], sum_grad, ROWS_T)
    base_ref[...] = dot(pre_grad, w_self_ref[...], COLS_T) + grads[pl.ds(0, rows_n)]
    rims_ref[...] = grads[pl.ds(rows_n, 2 * BLK)].astype(BF16)
    for p in range(peers_n):
        sends_ref[pl.ds(p * rows_n, rows_n)] = grads[pl.ds(halo * BLK + p * rows_n, rows_n)].astype(BF16)


def layer(recv, count, index, gathered, below, above, rows, tiles, degree, w_self, w_nbr, bias, cot, parts):
    blocks_n, links_n = index.shape
    peers_n, per_peer = recv.shape
    rows_n, width = rows.shape
    table_n = blocks_n + 2 + recv.size
    owners_n = blocks_n + 2 + peers_n * blocks_n
    plan = jnp.concatenate([recv.reshape(-1), count, index.reshape(-1)])
    smem = pl.BlockSpec(memory_space=pltpu.SMEM)
    hbm = pl.BlockSpec(memory_space=pl.ANY)
    vmem = pl.BlockSpec(memory_space=pltpu.VMEM)
    each = 2 * width * (width // BLK) // parts
    return pl.pallas_call(
        functools.partial(layer_kernel, blocks_n, links_n, peers_n, per_peer),
        out_shape=(
            jax.ShapeDtypeStruct((rows_n, width), BF16),
            jax.ShapeDtypeStruct((rows_n, width), F32),
            jax.ShapeDtypeStruct((2 * BLK, width), BF16),
            jax.ShapeDtypeStruct((peers_n * rows_n, width), BF16),
            jax.ShapeDtypeStruct((parts, 2 * each, BLK), BF16),
        ),
        in_specs=[smem] + [hbm] * 10,
        out_specs=(vmem,) * 5,
        scratch_shapes=[
            pltpu.VMEM(tiles.shape, BF16),
            pltpu.VMEM(degree.shape, degree.dtype),
            pltpu.VMEM(w_self.shape, BF16),
            pltpu.VMEM(w_nbr.shape, BF16),
            pltpu.VMEM(bias.shape, F32),
            pltpu.VMEM(cot.shape, BF16),
            pltpu.VMEM(((table_n + 1) * BLK, width), BF16),
            pltpu.VMEM(((owners_n + 1) * BLK, width), F32),
            pltpu.SemaphoreType.DMA((6,)),
            pltpu.SemaphoreType.DMA((blocks_n,)),
            pltpu.SemaphoreType.DMA((2 + recv.size,)),
        ],
        compiler_params=pltpu.CompilerParams(vmem_limit_bytes=56 * 2**20),
        cost_estimate=pl.CostEstimate(
            flops=1_300_000_000, bytes_accessed=12_000_000, transcendentals=rows_n * width
        ),
        name="layer",
    )(plan, gathered, below, above, rows, tiles, degree, w_self, w_nbr, bias, cot)


def shift(block_rows, axis, step):
    count = lax.axis_size(axis)
    pairs = [(i, i + step) for i in range(count) if 0 <= i + step < count]
    return lax.ppermute(block_rows, axis, pairs)


def swap(array, axis):
    return lax.all_to_all(array, axis, split_axis=0, concat_axis=0, tiled=True)


def on_device(
    features, send_list, nbr_count, nbr_index, tiles, degree, w_self, w_nbr, bias, cotangent
):
    rows = features[0]
    rows_n, width = rows.shape
    blocks_n = rows_n // BLK
    links_n = nbr_index.shape[-1]
    groups = lax.axis_size("grp")
    doms = lax.axis_size("dom")

    with jax.named_scope("gather_rows"):
        lists = jnp.pad(send_list.reshape(1, -1).astype(BF16), ((0, PAD - 1), (0, width - send_list.size)))
        wide = jnp.concatenate([rows, lists], axis=0).astype(F32) * SCALE
        packed = lax.all_gather(wide.astype(jnp.float16), "dom", tiled=True)
        gathered = (packed.astype(F32) * (1.0 / SCALE)).astype(BF16)
        lists = packed.reshape(doms, rows_n + PAD, width)[:, rows_n]
        slots = send_list.shape[-1]
        recv = lax.dynamic_slice_in_dim(lists, lax.axis_index("dom") * slots, slots, axis=1)
        recv = jnp.round(recv.astype(F32) * (1.0 / SCALE)).astype(jnp.int32)
    with jax.named_scope("rims"):
        below = shift(rows[rows_n - BLK :], "grp", 1)
        above = shift(rows[:BLK], "grp", -1)

    hidden, base, rims, sends, partial = layer(
        recv,
        nbr_count[0, 0],
        nbr_index[0, 0],
        gathered,
        below,
        above,
        rows,
        tiles.reshape(blocks_n * links_n, BLK, BLK),
        degree.reshape(blocks_n, BLK),
        w_self,
        w_nbr,
        bias.reshape(1, width),
        cotangent[0],
        groups,
    )

    with jax.named_scope("return_slots"):
        returned = lax.psum_scatter(sends, "dom", tiled=True)
    with jax.named_scope("return_rims"):
        from_above = shift(rims[:BLK], "grp", -1)
        from_below = shift(rims[BLK:], "grp", 1)
    with jax.named_scope("weight_sums"):
        chunk = jnp.sum(swap(partial, "grp").astype(F32), axis=0)
        chunk = jnp.sum(lax.all_gather(chunk, "dom"), axis=0)
        chunk = chunk * (1.0 / math.sqrt(rows_n * doms * groups))
        halves = width // BLK
        each = chunk.shape[0] // 2
        bias_grad = chunk[each : each + halves].reshape(width)
        finished = chunk[:each].astype(BF16)
        whole = swap(jnp.broadcast_to(finished[None], (groups, each, BLK)), "grp")
        whole = whole.reshape(halves, 2 * width, BLK).astype(F32)
        whole = jnp.concatenate([whole[i] for i in range(halves)], axis=1)
    edges = jnp.concatenate(
        [from_below, jnp.zeros((rows_n - 2 * BLK, width), BF16), from_above], axis=0
    )
    feat_grad = base + returned.astype(F32) + edges.astype(F32)
    return hidden[None], feat_grad[None], whole[:width], whole[width:], bias_grad


def solution(mesh):
    in_specs = (
        P("dom", "grp", None),
        P("dom", "grp", None, None),
        P("dom", "grp", None),
        P("dom", "grp", None, None),
        P("dom", "grp", None, None, None),
        P("dom", "grp"),
        P(),
        P(),
        P(),
        P("dom", "grp", None),
    )
    out_specs = (P("dom", "grp", None), P("dom", "grp", None), P(), P(), P())
    return jax.shard_map(
        on_device, mesh=mesh, in_specs=in_specs, out_specs=out_specs, check_vma=False
    )
```

```python
import functools
import math

import jax
import jax.numpy as jnp
from jax import lax
from jax.experimental import pallas as pl
from jax.experimental.pallas import tpu as pltpu
from jax.sharding import PartitionSpec as P

BLK = 128
PAD = 16
SCALE = 8192.0
F32 = jnp.float32
BF16 = jnp.bfloat16
ROWS_T = (((0,), (0,)), ((), ()))
COLS_T = (((1,), (1,)), ((), ()))


def dot(a, b, dims=(((1,), (0,)), ((), ()))):
    return lax.dot_general(a, b, dims, preferred_element_type=F32)


def block(t):
    return pl.ds(pl.multiple_of(t * BLK, BLK), BLK)


def layer_kernel(
    blocks_n,
    links_n,
    peers_n,
    per_peer,
    plan_ref,
    gathered_ref,
    below_ref,
    above_ref,
    rows_hbm,
    tiles_hbm,
    degree_hbm,
    w_self_hbm,
    w_nbr_hbm,
    bias_hbm,
    cot_hbm,
    hidden_ref,
    base_ref,
    to_above_ref,
    to_below_ref,
    slots_ref,
    *rest,
):
    parts_refs = rest[:-12]
    tiles_ref, degree_ref, w_self_ref, w_nbr_ref, bias_ref, cot_ref = rest[-12:-6]
    table, grads, weights = rest[-6:-3]
    own_sems, tile_sems, table_sems = rest[-3:]
    rows_n, width = cot_ref.shape
    halo = blocks_n + 2
    slots_n = peers_n * per_peer
    table_n = halo + slots_n
    rows_ref = table.at[pl.ds(0, rows_n)]
    own = [
        pltpu.make_async_copy(source, target, own_sems.at[i])
        for i, (source, target) in enumerate(
            (
                (rows_hbm, rows_ref),
                (w_self_hbm, w_self_ref),
                (degree_hbm, degree_ref),
                (bias_hbm, bias_ref),
                (w_nbr_hbm, w_nbr_ref),
                (cot_hbm, cot_ref),
            )
        )
    ]
    tile_copies = [
        pltpu.make_async_copy(
            tiles_hbm.at[pl.ds(b * links_n, links_n)],
            tiles_ref.at[pl.ds(b * links_n, links_n)],
            tile_sems.at[b],
        )
        for b in range(blocks_n)
    ]
    table_copies = []
    for slot in range(slots_n):
        source = (slot // per_peer) * (rows_n + PAD) + jnp.maximum(plan_ref[slot], 0) * BLK
        table_copies.append(
            pltpu.make_async_copy(
                gathered_ref.at[pl.ds(pl.multiple_of(source, PAD), BLK)],
                table.at[pl.ds((halo + slot) * BLK, BLK)],
                table_sems.at[slot],
            )
        )
    for copy in own + table_copies + tile_copies:
        copy.start()

    table[pl.ds(blocks_n * BLK, BLK)] = below_ref[...]
    table[pl.ds((blocks_n + 1) * BLK, BLK)] = above_ref[...]
    table[pl.ds(table_n * BLK, BLK)] = jnp.zeros((BLK, width), BF16)
    grads[...] = jnp.zeros_like(grads)
    entries = []
    for b in range(blocks_n):
        count = plan_ref[slots_n + b]
        for k in range(links_n):
            entry = plan_ref[slots_n + blocks_n + b * links_n + k]
            is_slot = entry >= halo
            slot = jnp.maximum(entry - halo, 0)
            dead = (k >= count) | (is_slot & (plan_ref[slot] < 0))
            entries.append(jnp.where(dead, table_n, entry))

    for copy in own:
        copy.wait()
    rows = rows_ref[...]
    self_act = dot(rows, w_self_ref[...]) + bias_ref[...]
    spreads = []
    for b in range(blocks_n):
        line = degree_ref[pl.ds(b, 1), :].astype(F32)
        column = jnp.transpose(jnp.broadcast_to(line, (BLK, BLK)))
        spreads.append(jnp.concatenate([column] * (width // BLK), axis=1))
    for copy in table_copies:
        copy.wait()

    means = []
    for b in range(blocks_n):
        tile_copies[b].wait()
        total = None
        for k in range(0, links_n, 2):
            at = b * links_n + k
            left = jnp.concatenate([tiles_ref[at], tiles_ref[at + 1]], axis=1)
            right = jnp.concatenate([table[block(entries[at])], table[block(entries[at + 1])]], axis=0)
            term = dot(left, right)
            total = term if total is None else total + term
        means.append((total / spreads[b]).astype(BF16))
    mean_rows = jnp.concatenate(means, axis=0)
    pre_act = self_act + dot(mean_rows, w_nbr_ref[...])
    gate = jax.nn.sigmoid(pre_act)
    hidden_ref[...] = (pre_act * gate).astype(BF16)
    slope = gate * (1.0 + pre_act * (1.0 - gate))
    pre_grad = (cot_ref[...].astype(F32) * slope).astype(BF16)
    grad_all = jnp.concatenate([dot(rows, pre_grad, ROWS_T), dot(mean_rows, pre_grad, ROWS_T)], axis=0)
    bias_sum = jnp.sum(pre_grad.astype(F32), axis=0, keepdims=True)
    bias_rows = jnp.concatenate([bias_sum, jnp.zeros((PAD - 1, width), F32)], axis=0).astype(BF16)
    weights[...] = grad_all
    parts = len(parts_refs)
    each = 2 * width // parts
    mine = plan_ref[slots_n + blocks_n + blocks_n * links_n]
    for step, part_ref in enumerate(parts_refs):
        start = pl.multiple_of(lax.rem(mine + step, parts) * each, each)
        part_ref[pl.ds(0, each)] = weights[pl.ds(start, each)].astype(BF16)
        part_ref[pl.ds(each, PAD)] = bias_rows

    mean_grad = dot(pre_grad, w_nbr_ref[...], COLS_T)
    for b in range(blocks_n):
        sum_grad = (mean_grad[b * BLK : (b + 1) * BLK] / spreads[b]).astype(BF16)
        for k in range(links_n):
            at = b * links_n + k
            where = block(entries[at])
            grads[where] += dot(tiles_ref[at], sum_grad, ROWS_T)
    base_ref[...] = dot(pre_grad, w_self_ref[...], COLS_T) + grads[pl.ds(0, rows_n)]
    to_below_ref[...] = grads[pl.ds(rows_n, BLK)].astype(BF16)
    to_above_ref[...] = grads[pl.ds(rows_n + BLK, BLK)].astype(BF16)
    for slot in range(slots_n):
        slots_ref[pl.ds(slot * BLK, BLK)] = grads[pl.ds((halo + slot) * BLK, BLK)].astype(BF16)


def layer(recv, count, index, mine, gathered, below, above, rows, tiles, degree, w_self, w_nbr, bias, cot, parts):
    blocks_n, links_n = index.shape
    peers_n, per_peer = recv.shape
    rows_n, width = rows.shape
    table_n = blocks_n + 2 + recv.size
    plan = jnp.concatenate([recv.reshape(-1), count, index.reshape(-1), mine.reshape(1)])
    smem = pl.BlockSpec(memory_space=pltpu.SMEM)
    hbm = pl.BlockSpec(memory_space=pl.ANY)
    vmem = pl.BlockSpec(memory_space=pltpu.VMEM)
    each = 2 * width // parts
    outs = [
        jax.ShapeDtypeStruct((rows_n, width), BF16),
        jax.ShapeDtypeStruct((rows_n, width), F32),
        jax.ShapeDtypeStruct((BLK, width), BF16),
        jax.ShapeDtypeStruct((BLK, width), BF16),
        jax.ShapeDtypeStruct((recv.size * BLK, width), BF16),
    ] + [jax.ShapeDtypeStruct((each + PAD, width), BF16)] * parts
    return pl.pallas_call(
        functools.partial(layer_kernel, blocks_n, links_n, peers_n, per_peer),
        out_shape=outs,
        in_specs=[smem, hbm, vmem, vmem] + [hbm] * 7,
        out_specs=[vmem] * len(outs),
        scratch_shapes=[
            pltpu.VMEM(tiles.shape, BF16),
            pltpu.VMEM(degree.shape, degree.dtype),
            pltpu.VMEM(w_self.shape, BF16),
            pltpu.VMEM(w_nbr.shape, BF16),
            pltpu.VMEM(bias.shape, F32),
            pltpu.VMEM(cot.shape, BF16),
            pltpu.VMEM(((table_n + 1) * BLK, width), BF16),
            pltpu.VMEM(((table_n + 1) * BLK, width), F32),
            pltpu.VMEM((2 * width, width), F32),
            pltpu.SemaphoreType.DMA((6,)),
            pltpu.SemaphoreType.DMA((blocks_n,)),
            pltpu.SemaphoreType.DMA((recv.size,)),
        ],
        compiler_params=pltpu.CompilerParams(vmem_limit_bytes=56 * 2**20),
        cost_estimate=pl.CostEstimate(
            flops=1_300_000_000, bytes_accessed=12_000_000, transcendentals=rows_n * width
        ),
        name="layer",
    )(plan, gathered, below, above, rows, tiles, degree, w_self, w_nbr, bias, cot)


def collect_kernel(blocks_n, sent_ref, base_ref, returned_ref, below_ref, above_ref, out_ref, total):
    rows_n, width = base_ref.shape
    total[pl.ds(0, rows_n)] = base_ref[...]
    total[pl.ds(rows_n, BLK)] = jnp.zeros((BLK, width), F32)
    total[pl.ds(0, BLK)] += below_ref[...].astype(F32)
    total[pl.ds(rows_n - BLK, BLK)] += above_ref[...].astype(F32)
    peers_n, per_peer = sent_ref.shape
    for p in range(peers_n):
        for s in range(per_peer):
            owner = sent_ref[p, s]
            where = block(jnp.where(owner < 0, blocks_n, owner))
            total[where] += returned_ref[pl.ds((p * per_peer + s) * BLK, BLK)].astype(F32)
    out_ref[...] = total[pl.ds(0, rows_n)]


def collect(sent, base, returned, below, above):
    rows_n, width = base.shape
    smem = pl.BlockSpec(memory_space=pltpu.SMEM)
    vmem = pl.BlockSpec(memory_space=pltpu.VMEM)
    return pl.pallas_call(
        functools.partial(collect_kernel, rows_n // BLK),
        out_shape=jax.ShapeDtypeStruct((rows_n, width), F32),
        in_specs=[smem] + [vmem] * 4,
        out_specs=vmem,
        scratch_shapes=[pltpu.VMEM((rows_n + BLK, width), F32)],
        compiler_params=pltpu.CompilerParams(vmem_limit_bytes=16 * 2**20),
        cost_estimate=pl.CostEstimate(flops=5_000_000, bytes_accessed=4_000_000, transcendentals=0),
        name="collect",
    )(sent, base, returned, below, above)


def assemble_kernel(mine_ref, *refs):
    *pieces, self_ref, nbr_ref, whole = refs
    each, width = pieces[0].shape
    parts = len(pieces)
    for step, piece in enumerate(pieces):
        start = lax.rem(mine_ref[0] + parts - step, parts) * each
        whole[pl.ds(pl.multiple_of(start, each), each)] = piece[...].astype(F32)
    self_ref[...] = whole[pl.ds(0, width)]
    nbr_ref[...] = whole[pl.ds(width, width)]


def assemble(mine, pieces):
    width = pieces[0].shape[1]
    smem = pl.BlockSpec(memory_space=pltpu.SMEM)
    vmem = pl.BlockSpec(memory_space=pltpu.VMEM)
    return pl.pallas_call(
        assemble_kernel,
        out_shape=(jax.ShapeDtypeStruct((width, width), F32),) * 2,
        in_specs=[smem] + [vmem] * len(pieces),
        out_specs=(vmem,) * 2,
        scratch_shapes=[pltpu.VMEM((2 * width, width), F32)],
        compiler_params=pltpu.CompilerParams(vmem_limit_bytes=8 * 2**20),
        cost_estimate=pl.CostEstimate(flops=0, bytes_accessed=1_000_000, transcendentals=0),
        name="assemble",
    )(mine.reshape(1), *pieces)


def rotation_sum(terms):
    terms = [term.astype(F32) for term in terms]
    while len(terms) > 1:
        half = len(terms) // 2
        terms = [terms[i] + terms[i + half] for i in range(half)]
    return terms[0]


def shift(block_rows, axis, step):
    count = lax.axis_size(axis)
    pairs = [(i, i + step) for i in range(count) if 0 <= i + step < count]
    return lax.ppermute(block_rows, axis, pairs)


def swap(array, axis):
    return lax.all_to_all(array, axis, split_axis=0, concat_axis=0, tiled=True)


def on_device(
    features, send_list, nbr_count, nbr_index, tiles, degree, w_self, w_nbr, bias, cotangent
):
    rows = features[0]
    rows_n, width = rows.shape
    blocks_n = rows_n // BLK
    links_n = nbr_index.shape[-1]
    groups = lax.axis_size("grp")
    doms = lax.axis_size("dom")

    with jax.named_scope("gather_rows"):
        lists = jnp.pad(send_list.reshape(1, -1).astype(BF16), ((0, PAD - 1), (0, width - send_list.size)))
        wide = jnp.concatenate([rows, lists], axis=0).astype(F32) * SCALE
        packed = lax.all_gather(wide.astype(jnp.float16), "dom", tiled=True)
        gathered = (packed.astype(F32) * (1.0 / SCALE)).astype(BF16)
        lists = packed.reshape(doms, rows_n + PAD, width)[:, rows_n]
        slots = send_list.shape[-1]
        recv = lax.dynamic_slice_in_dim(lists, lax.axis_index("dom") * slots, slots, axis=1)
        recv = jnp.round(recv.astype(F32) * (1.0 / SCALE)).astype(jnp.int32)
    with jax.named_scope("rims"):
        below = shift(rows[rows_n - BLK :], "grp", 1)
        above = shift(rows[:BLK], "grp", -1)

    inner = 1 << ((groups.bit_length()) // 2)
    outer = groups // inner

    def turn(array, far, near):
        pairs = [
            (y * inner + z, (y + far) % outer * inner + (z + near) % inner)
            for y in range(outer)
            for z in range(inner)
        ]
        return lax.ppermute(array, "grp", pairs)

    mine = lax.rem(lax.axis_index("grp"), inner)
    hidden, base, to_above, to_below, slot_grads, *partial = layer(
        recv,
        nbr_count[0, 0],
        nbr_index[0, 0],
        mine,
        gathered,
        below,
        above,
        rows,
        tiles.reshape(blocks_n * links_n, BLK, BLK),
        degree.reshape(blocks_n, BLK),
        w_self,
        w_nbr,
        bias.reshape(1, width),
        cotangent[0],
        inner,
    )

    with jax.named_scope("return_slots"):
        returned = swap(slot_grads, "dom")
    with jax.named_scope("return_rims"):
        from_above = shift(to_below, "grp", -1)
        from_below = shift(to_above, "grp", 1)
    with jax.named_scope("weight_sums"):
        chunk = rotation_sum([partial[0]] + [turn(partial[k], 0, k) for k in range(1, inner)])
        chunk = chunk.astype(BF16)
        chunk = rotation_sum([chunk] + [turn(chunk, k, 0) for k in range(1, outer)])
        chunk = lax.all_gather(chunk.astype(BF16), "dom").astype(F32)
        chunk = jnp.sum(chunk, axis=0) * (1.0 / math.sqrt(rows_n * doms * groups))
        bias_grad = chunk[chunk.shape[0] - PAD]
        chunk = chunk[: chunk.shape[0] - PAD].astype(BF16)
        pieces = [chunk] + [turn(chunk, 0, k) for k in range(1, inner)]
        grad_self, grad_nbr = assemble(mine, pieces)
    feat_grad = collect(send_list[0, 0], base, returned, from_below, from_above)
    return hidden[None], feat_grad[None], grad_self, grad_nbr, bias_grad


def solution(mesh):
    in_specs = (
        P("dom", "grp", None),
        P("dom", "grp", None, None),
        P("dom", "grp", None),
        P("dom", "grp", None, None),
        P("dom", "grp", None, None, None),
        P("dom", "grp"),
        P(),
        P(),
        P(),
        P("dom", "grp", None),
    )
    out_specs = (P("dom", "grp", None), P("dom", "grp", None), P(), P(), P())
    return jax.shard_map(
        on_device, mesh=mesh, in_specs=in_specs, out_specs=out_specs, check_vma=False
    )
```

```python
import functools
import math

import jax
import jax.numpy as jnp
from jax import lax
from jax.experimental import pallas as pl
from jax.experimental.pallas import tpu as pltpu
from jax.sharding import PartitionSpec as P

BLK = 128
PAD = 16
SCALE = 8192.0
F32 = jnp.float32
BF16 = jnp.bfloat16
ROWS_T = (((0,), (0,)), ((), ()))
COLS_T = (((1,), (1,)), ((), ()))


def dot(a, b, dims=(((1,), (0,)), ((), ()))):
    return lax.dot_general(a, b, dims, preferred_element_type=F32)


def block(t):
    return pl.ds(pl.multiple_of(t * BLK, BLK), BLK)


def live_entries(plan_ref, blocks_n, links_n, peers_n, per_peer):
    halo = blocks_n + 2
    slots_n = peers_n * per_peer
    entries = []
    for b in range(blocks_n):
        count = plan_ref[slots_n + b]
        for k in range(links_n):
            entry = plan_ref[slots_n + blocks_n + b * links_n + k]
            slot = jnp.maximum(entry - halo, 0)
            dead = (k >= count) | ((entry >= halo) & (plan_ref[slot] < 0))
            entries.append(jnp.where(dead, halo + slots_n, entry))
    return entries


def column_spread(degree_ref, b, width):
    line = degree_ref[pl.ds(b, 1), :].astype(F32)
    column = jnp.transpose(jnp.broadcast_to(line, (BLK, BLK)))
    return jnp.concatenate([column] * (width // BLK), axis=1)


def layer_kernel(
    blocks_n,
    links_n,
    peers_n,
    per_peer,
    plan_ref,
    gathered_ref,
    below_ref,
    above_ref,
    rows_hbm,
    tiles_hbm,
    degree_hbm,
    w_self_hbm,
    w_nbr_hbm,
    bias_hbm,
    cot_hbm,
    hidden_ref,
    self_grad_ref,
    sum_grad_ref,
    weights_ref,
    tiles_ref,
    degree_ref,
    w_self_ref,
    w_nbr_ref,
    bias_ref,
    cot_ref,
    table,
    own_sems,
    tile_sems,
    table_sems,
):
    rows_n, width = cot_ref.shape
    halo = blocks_n + 2
    slots_n = peers_n * per_peer
    table_n = halo + slots_n
    rows_ref = table.at[pl.ds(0, rows_n)]
    own = [
        pltpu.make_async_copy(source, target, own_sems.at[i])
        for i, (source, target) in enumerate(
            (
                (rows_hbm, rows_ref),
                (w_self_hbm, w_self_ref),
                (degree_hbm, degree_ref),
                (bias_hbm, bias_ref),
                (w_nbr_hbm, w_nbr_ref),
                (cot_hbm, cot_ref),
            )
        )
    ]
    tile_copies = [
        pltpu.make_async_copy(
            tiles_hbm.at[pl.ds(b * links_n, links_n)],
            tiles_ref.at[pl.ds(b * links_n, links_n)],
            tile_sems.at[b],
        )
        for b in range(blocks_n)
    ]
    table_copies = []
    for slot in range(slots_n):
        source = (slot // per_peer) * (rows_n + PAD) + jnp.maximum(plan_ref[slot], 0) * BLK
        table_copies.append(
            pltpu.make_async_copy(
                gathered_ref.at[pl.ds(pl.multiple_of(source, PAD), BLK)],
                table.at[pl.ds((halo + slot) * BLK, BLK)],
                table_sems.at[slot],
            )
        )
    for copy in own + table_copies + tile_copies:
        copy.start()

    table[pl.ds(blocks_n * BLK, BLK)] = below_ref[...]
    table[pl.ds((blocks_n + 1) * BLK, BLK)] = above_ref[...]
    table[pl.ds(table_n * BLK, BLK)] = jnp.zeros((BLK, width), BF16)
    entries = live_entries(plan_ref, blocks_n, links_n, peers_n, per_peer)

    for copy in own:
        copy.wait()
    rows = rows_ref[...]
    self_act = dot(rows, w_self_ref[...]) + bias_ref[...]
    spreads = [column_spread(degree_ref, b, width) for b in range(blocks_n)]
    for copy in table_copies:
        copy.wait()

    means = []
    for b in range(blocks_n):
        tile_copies[b].wait()
        total = None
        for k in range(0, links_n, 2):
            at = b * links_n + k
            left = jnp.concatenate([tiles_ref[at], tiles_ref[at + 1]], axis=1)
            right = jnp.concatenate([table[block(entries[at])], table[block(entries[at + 1])]], axis=0)
            term = dot(left, right)
            total = term if total is None else total + term
        means.append((total / spreads[b]).astype(BF16))
    mean_rows = jnp.concatenate(means, axis=0)
    pre_act = self_act + dot(mean_rows, w_nbr_ref[...])
    gate = jax.nn.sigmoid(pre_act)
    hidden_ref[...] = (pre_act * gate).astype(BF16)
    slope = gate * (1.0 + pre_act * (1.0 - gate))
    pre_grad = (cot_ref[...].astype(F32) * slope).astype(BF16)

    grad_all = jnp.concatenate([dot(rows, pre_grad, ROWS_T), dot(mean_rows, pre_grad, ROWS_T)], axis=0)
    grad_all = grad_all.astype(BF16)
    bias_sum = jnp.sum(pre_grad.astype(F32), axis=0, keepdims=True)
    bias_rows = jnp.concatenate([bias_sum, jnp.zeros((PAD - 1, width), F32)], axis=0).astype(BF16)
    parts = weights_ref.shape[0]
    each = 2 * width // parts
    for part in range(parts):
        weights_ref[part, pl.ds(0, each)] = grad_all[part * each : (part + 1) * each]
        weights_ref[part, pl.ds(each, PAD)] = bias_rows

    self_grad_ref[...] = dot(pre_grad, w_self_ref[...], COLS_T)
    mean_grad = dot(pre_grad, w_nbr_ref[...], COLS_T)
    for b in range(blocks_n):
        part = mean_grad[b * BLK : (b + 1) * BLK] / spreads[b]
        sum_grad_ref[pl.ds(b * BLK, BLK)] = part.astype(BF16)


def layer(dims, plan, gathered, below, above, rows, tiles, degree, w_self, w_nbr, bias, cot, parts):
    blocks_n, links_n, peers_n, per_peer = dims
    slots_n = peers_n * per_peer
    rows_n, width = rows.shape
    table_n = blocks_n + 2 + slots_n
    smem = pl.BlockSpec(memory_space=pltpu.SMEM)
    hbm = pl.BlockSpec(memory_space=pl.ANY)
    vmem = pl.BlockSpec(memory_space=pltpu.VMEM)
    return pl.pallas_call(
        functools.partial(layer_kernel, *dims),
        out_shape=(
            jax.ShapeDtypeStruct((rows_n, width), BF16),
            jax.ShapeDtypeStruct((rows_n, width), F32),
            jax.ShapeDtypeStruct((rows_n, width), BF16),
            jax.ShapeDtypeStruct((parts, 2 * width // parts + PAD, width), BF16),
        ),
        in_specs=[smem, hbm, vmem, vmem] + [hbm] * 7,
        out_specs=(vmem,) * 4,
        scratch_shapes=[
            pltpu.VMEM(tiles.shape, BF16),
            pltpu.VMEM(degree.shape, degree.dtype),
            pltpu.VMEM(w_self.shape, BF16),
            pltpu.VMEM(w_nbr.shape, BF16),
            pltpu.VMEM(bias.shape, F32),
            pltpu.VMEM(cot.shape, BF16),
            pltpu.VMEM(((table_n + 1) * BLK, width), BF16),
            pltpu.SemaphoreType.DMA((6,)),
            pltpu.SemaphoreType.DMA((blocks_n,)),
            pltpu.SemaphoreType.DMA((slots_n,)),
        ],
        compiler_params=pltpu.CompilerParams(vmem_limit_bytes=56 * 2**20),
        cost_estimate=pl.CostEstimate(
            flops=800_000_000, bytes_accessed=8_000_000, transcendentals=rows_n * width
        ),
        name="layer",
    )(plan, gathered, below, above, rows, tiles, degree, w_self, w_nbr, bias, cot)


def links_kernel(
    blocks_n,
    links_n,
    peers_n,
    per_peer,
    plan_ref,
    tiles_hbm,
    self_grad_ref,
    sum_grad_ref,
    base_ref,
    to_above_ref,
    to_below_ref,
    slots_ref,
    tiles_ref,
    grads,
    tile_sems,
):
    rows_n, width = base_ref.shape
    halo = blocks_n + 2
    slots_n = peers_n * per_peer
    tile_copies = [
        pltpu.make_async_copy(
            tiles_hbm.at[pl.ds(b * links_n, links_n)],
            tiles_ref.at[pl.ds(b * links_n, links_n)],
            tile_sems.at[b],
        )
        for b in range(blocks_n)
    ]
    for copy in tile_copies:
        copy.start()
    grads[...] = jnp.zeros_like(grads)
    entries = live_entries(plan_ref, blocks_n, links_n, peers_n, per_peer)
    for b in range(blocks_n):
        tile_copies[b].wait()
        sum_grad = sum_grad_ref[pl.ds(b * BLK, BLK)]
        for k in range(links_n):
            at = b * links_n + k
            where = block(entries[at])
            grads[where] += dot(tiles_ref[at], sum_grad, ROWS_T)
    base_ref[...] = self_grad_ref[...] + grads[pl.ds(0, rows_n)]
    to_below_ref[...] = grads[pl.ds(rows_n, BLK)].astype(BF16)
    to_above_ref[...] = grads[pl.ds(rows_n + BLK, BLK)].astype(BF16)
    for slot in range(slots_n):
        slots_ref[pl.ds(slot * BLK, BLK)] = grads[pl.ds((halo + slot) * BLK, BLK)].astype(BF16)


def links(dims, plan, tiles, self_grad, sum_grad):
    blocks_n, links_n, peers_n, per_peer = dims
    slots_n = peers_n * per_peer
    rows_n, width = self_grad.shape
    table_n = blocks_n + 2 + slots_n
    smem = pl.BlockSpec(memory_space=pltpu.SMEM)
    hbm = pl.BlockSpec(memory_space=pl.ANY)
    vmem = pl.BlockSpec(memory_space=pltpu.VMEM)
    return pl.pallas_call(
        functools.partial(links_kernel, *dims),
        out_shape=(
            jax.ShapeDtypeStruct((rows_n, width), F32),
            jax.ShapeDtypeStruct((BLK, width), BF16),
            jax.ShapeDtypeStruct((BLK, width), BF16),
            jax.ShapeDtypeStruct((slots_n * BLK, width), BF16),
        ),
        in_specs=[smem, hbm, vmem, vmem],
        out_specs=(vmem,) * 4,
        scratch_shapes=[
            pltpu.VMEM(tiles.shape, BF16),
            pltpu.VMEM(((table_n + 1) * BLK, width), F32),
            pltpu.SemaphoreType.DMA((blocks_n,)),
        ],
        compiler_params=pltpu.CompilerParams(vmem_limit_bytes=56 * 2**20),
        cost_estimate=pl.CostEstimate(flops=400_000_000, bytes_accessed=6_000_000, transcendentals=0),
        name="links",
    )(plan, tiles, self_grad, sum_grad)


def collect_kernel(blocks_n, sent_ref, base_ref, returned_ref, below_ref, above_ref, out_ref, total):
    rows_n, width = base_ref.shape
    total[pl.ds(0, rows_n)] = base_ref[...]
    total[pl.ds(rows_n, BLK)] = jnp.zeros((BLK, width), F32)
    total[pl.ds(0, BLK)] += below_ref[...].astype(F32)
    total[pl.ds(rows_n - BLK, BLK)] += above_ref[...].astype(F32)
    peers_n, per_peer = sent_ref.shape
    for p in range(peers_n):
        for s in range(per_peer):
            owner = sent_ref[p, s]
            where = block(jnp.where(owner < 0, blocks_n, owner))
            total[where] += returned_ref[pl.ds((p * per_peer + s) * BLK, BLK)].astype(F32)
    out_ref[...] = total[pl.ds(0, rows_n)]


def collect(sent, base, returned, below, above):
    rows_n, width = base.shape
    smem = pl.BlockSpec(memory_space=pltpu.SMEM)
    vmem = pl.BlockSpec(memory_space=pltpu.VMEM)
    return pl.pallas_call(
        functools.partial(collect_kernel, rows_n // BLK),
        out_shape=jax.ShapeDtypeStruct((rows_n, width), F32),
        in_specs=[smem] + [vmem] * 4,
        out_specs=vmem,
        scratch_shapes=[pltpu.VMEM((rows_n + BLK, width), F32)],
        compiler_params=pltpu.CompilerParams(vmem_limit_bytes=16 * 2**20),
        cost_estimate=pl.CostEstimate(flops=5_000_000, bytes_accessed=4_000_000, transcendentals=0),
        name="collect",
    )(sent, base, returned, below, above)


def row_sum(terms):
    terms = [terms[i].astype(F32) for i in range(terms.shape[0])]
    while len(terms) > 1:
        terms = [terms[i] + terms[i + 1] for i in range(0, len(terms), 2)]
    return terms[0]


def shift(block_rows, axis, step):
    count = lax.axis_size(axis)
    pairs = [(i, i + step) for i in range(count) if 0 <= i + step < count]
    return lax.ppermute(block_rows, axis, pairs)


def swap(array, axis, rings=None):
    return lax.all_to_all(
        array, axis, split_axis=0, concat_axis=0, tiled=True, axis_index_groups=rings
    )


def on_device(
    features, send_list, nbr_count, nbr_index, tiles, degree, w_self, w_nbr, bias, cotangent
):
    rows = features[0]
    rows_n, width = rows.shape
    blocks_n = rows_n // BLK
    links_n = nbr_index.shape[-1]
    groups = lax.axis_size("grp")
    doms = lax.axis_size("dom")

    with jax.named_scope("gather_rows"):
        slots = send_list.shape[-1]
        lists = jnp.pad(send_list[0, 0].T.astype(BF16), ((0, PAD - slots), (0, width - doms)))
        wide = jnp.concatenate([rows, lists], axis=0).astype(F32) * SCALE
        packed = lax.all_gather(wide.astype(jnp.float16), "dom", tiled=True)
        gathered = (packed.astype(F32) * (1.0 / SCALE)).astype(BF16)
        lists = packed.reshape(doms, rows_n + PAD, width)[:, rows_n : rows_n + slots]
        recv = lax.dynamic_slice_in_dim(lists, lax.axis_index("dom"), 1, axis=2)
        recv = jnp.round(recv.astype(F32) * (1.0 / SCALE)).astype(jnp.int32)
    with jax.named_scope("rims"):
        below = shift(rows[rows_n - BLK :], "grp", 1)
        above = shift(rows[:BLK], "grp", -1)

    inner = 1 << ((groups.bit_length()) // 2)
    outer = groups // inner

    rings_z = [[y * inner + z for z in range(inner)] for y in range(outer)]
    rings_y = [[y * inner + z for y in range(outer)] for z in range(inner)]
    dims = (blocks_n, links_n, doms, slots)
    plan = jnp.concatenate([recv.reshape(-1), nbr_count.reshape(-1), nbr_index.reshape(-1)])
    flat_tiles = tiles.reshape(blocks_n * links_n, BLK, BLK)
    hidden, self_grad, sum_grad, partial = layer(
        dims,
        plan,
        gathered,
        below,
        above,
        rows,
        flat_tiles,
        degree.reshape(blocks_n, BLK),
        w_self,
        w_nbr,
        bias.reshape(1, width),
        cotangent[0],
        inner,
    )
    with jax.named_scope("weight_sums_z"):
        chunk = swap(partial, "grp", rings_z)
    base, to_above, to_below, slot_grads = links(dims, plan, flat_tiles, self_grad, sum_grad)
    with jax.named_scope("weight_sums"):
        chunk = row_sum(chunk).astype(BF16)
        chunk, slot_grads = lax.optimization_barrier((chunk, slot_grads))
    with jax.named_scope("return_slots"):
        returned = swap(slot_grads, "dom")
    with jax.named_scope("return_rims"):
        from_above = shift(to_below, "grp", -1)
        from_below = shift(to_above, "grp", 1)
    with jax.named_scope("weight_sums"):
        chunk = row_sum(lax.all_gather(chunk, "grp", axis_index_groups=rings_y)).astype(BF16)
        chunk = row_sum(lax.all_gather(chunk, "dom"))
        chunk = chunk * (1.0 / math.sqrt(rows_n * doms * groups))
        each = chunk.shape[0] - PAD
        bias_grad = chunk[each]
        finished, returned = lax.optimization_barrier((chunk[:each].astype(BF16), returned))
        whole = jnp.broadcast_to(finished[None], (inner, each, width))
        whole = swap(whole, "grp", rings_z).reshape(2 * width, width).astype(F32)
    feat_grad = collect(send_list[0, 0], base, returned, from_below, from_above)
    return hidden[None], feat_grad[None], whole[:width], whole[width:], bias_grad


def solution(mesh):
    in_specs = (
        P("dom", "grp", None),
        P("dom", "grp", None, None),
        P("dom", "grp", None),
        P("dom", "grp", None, None),
        P("dom", "grp", None, None, None),
        P("dom", "grp"),
        P(),
        P(),
        P(),
        P("dom", "grp", None),
    )
    out_specs = (P("dom", "grp", None), P("dom", "grp", None), P(), P(), P())
    return jax.shard_map(
        on_device, mesh=mesh, in_specs=in_specs, out_specs=out_specs, check_vma=False
    )
```

```python
import functools
import math

import jax
import jax.numpy as jnp
from jax import lax
from jax.experimental import pallas as pl
from jax.experimental.pallas import tpu as pltpu
from jax.sharding import Mesh
from jax.sharding import PartitionSpec as P

BLK = 128
PAD = 16
SCALE = 8192.0
GRP = ("hi", "lo")
F32 = jnp.float32
BF16 = jnp.bfloat16
ROWS_T = (((0,), (0,)), ((), ()))
COLS_T = (((1,), (1,)), ((), ()))


def dot(a, b, dims=(((1,), (0,)), ((), ()))):
    return lax.dot_general(a, b, dims, preferred_element_type=F32)


def block(t):
    return pl.ds(pl.multiple_of(t * BLK, BLK), BLK)


def layer_kernel(
    blocks_n,
    links_n,
    peers_n,
    per_peer,
    plan_ref,
    gathered_ref,
    below_ref,
    above_ref,
    rows_hbm,
    tiles_hbm,
    degree_hbm,
    w_self_hbm,
    w_nbr_hbm,
    bias_hbm,
    cot_hbm,
    hidden_ref,
    base_ref,
    rims_ref,
    keep_ref,
    give_ref,
    mean_ref,
    pre_grad_ref,
    tiles_ref,
    degree_ref,
    w_self_ref,
    w_nbr_ref,
    bias_ref,
    cot_ref,
    table,
    grads,
    own_sems,
    tile_sems,
    table_sems,
):
    rows_n, width = cot_ref.shape
    halo = blocks_n + 2
    slots_n = peers_n * per_peer
    table_n = halo + slots_n
    rows_ref = table.at[pl.ds(0, rows_n)]
    own = [
        pltpu.make_async_copy(source, target, own_sems.at[i])
        for i, (source, target) in enumerate(
            (
                (rows_hbm, rows_ref),
                (w_self_hbm, w_self_ref),
                (degree_hbm, degree_ref),
                (bias_hbm, bias_ref),
                (w_nbr_hbm, w_nbr_ref),
                (cot_hbm, cot_ref),
            )
        )
    ]
    tile_copies = [
        pltpu.make_async_copy(
            tiles_hbm.at[pl.ds(b * links_n, links_n)],
            tiles_ref.at[pl.ds(b * links_n, links_n)],
            tile_sems.at[b],
        )
        for b in range(blocks_n)
    ]
    table_copies = [
        pltpu.make_async_copy(below_ref, table.at[pl.ds(blocks_n * BLK, BLK)], table_sems.at[0]),
        pltpu.make_async_copy(above_ref, table.at[pl.ds((blocks_n + 1) * BLK, BLK)], table_sems.at[1]),
    ]
    for slot in range(slots_n):
        source = (slot // per_peer) * (rows_n + PAD) + jnp.maximum(plan_ref[slot], 0) * BLK
        table_copies.append(
            pltpu.make_async_copy(
                gathered_ref.at[pl.ds(pl.multiple_of(source, PAD), BLK)],
                table.at[pl.ds((halo + slot) * BLK, BLK)],
                table_sems.at[2 + slot],
            )
        )
    for copy in own + table_copies + tile_copies:
        copy.start()

    table[pl.ds(table_n * BLK, BLK)] = jnp.zeros((BLK, width), BF16)
    grads[...] = jnp.zeros_like(grads)
    entries = []
    owners = []
    for b in range(blocks_n):
        count = plan_ref[slots_n + b]
        for k in range(links_n):
            entry = plan_ref[slots_n + blocks_n + b * links_n + k]
            is_slot = entry >= halo
            slot = jnp.maximum(entry - halo, 0)
            owner = plan_ref[slot]
            dead = (k >= count) | (is_slot & (owner < 0))
            entries.append(jnp.where(dead, table_n, entry))
            owner = jnp.where(is_slot, halo + (slot // per_peer) * blocks_n + owner, entry)
            owners.append(jnp.where(dead, halo + peers_n * blocks_n, owner))

    for copy in own:
        copy.wait()
    rows = rows_ref[...]
    self_act = dot(rows, w_self_ref[...]) + bias_ref[...]
    spreads = []
    for b in range(blocks_n):
        line = degree_ref[pl.ds(b, 1), :].astype(F32)
        column = jnp.transpose(jnp.broadcast_to(line, (BLK, BLK)))
        spreads.append(jnp.concatenate([column] * (width // BLK), axis=1))
    for copy in table_copies:
        copy.wait()

    means = []
    for b in range(blocks_n):
        tile_copies[b].wait()
        total = None
        for k in range(0, links_n, 2):
            at = b * links_n + k
            left = jnp.concatenate([tiles_ref[at], tiles_ref[at + 1]], axis=1)
            right = jnp.concatenate([table[block(entries[at])], table[block(entries[at + 1])]], axis=0)
            term = dot(left, right)
            total = term if total is None else total + term
        means.append((total / spreads[b]).astype(BF16))
    mean_rows = jnp.concatenate(means, axis=0)
    pre_act = self_act + dot(mean_rows, w_nbr_ref[...])
    gate = jax.nn.sigmoid(pre_act)
    hidden_ref[...] = (pre_act * gate).astype(BF16)
    slope = gate * (1.0 + pre_act * (1.0 - gate))
    pre_grad = (cot_ref[...].astype(F32) * slope).astype(BF16)
    mean_ref[...] = mean_rows
    pre_grad_ref[...] = pre_grad

    mean_grad = dot(pre_grad, w_nbr_ref[...], COLS_T)
    for b in range(blocks_n):
        sum_grad = (mean_grad[b * BLK : (b + 1) * BLK] / spreads[b]).astype(BF16)
        for k in range(links_n):
            at = b * links_n + k
            where = block(owners[at])
            grads[where] += dot(tiles_ref[at], sum_grad, ROWS_T)
    base_ref[...] = dot(pre_grad, w_self_ref[...], COLS_T) + grads[pl.ds(0, rows_n)]
    rims_ref[...] = grads[pl.ds(rows_n, 2 * BLK)].astype(BF16)
    core = plan_ref[slots_n + blocks_n + blocks_n * links_n]
    for chip in range(peers_n // 2):
        here = pl.ds(chip * rows_n, rows_n)
        for target, side in ((give_ref, 1 - core), (keep_ref, core)):
            start = halo * BLK + (2 * chip + side) * rows_n
            target[here] = grads[pl.ds(pl.multiple_of(start, BLK), rows_n)].astype(BF16)


def layer(recv, count, index, core, gathered, below, above, rows, tiles, degree, w_self, w_nbr, bias, cot):
    blocks_n, links_n = index.shape
    peers_n, per_peer = recv.shape
    rows_n, width = rows.shape
    table_n = blocks_n + 2 + recv.size
    owners_n = blocks_n + 2 + peers_n * blocks_n
    plan = jnp.concatenate([recv.reshape(-1), count, index.reshape(-1), core.reshape(1)])
    smem = pl.BlockSpec(memory_space=pltpu.SMEM)
    hbm = pl.BlockSpec(memory_space=pl.ANY)
    vmem = pl.BlockSpec(memory_space=pltpu.VMEM)
    return pl.pallas_call(
        functools.partial(layer_kernel, blocks_n, links_n, peers_n, per_peer),
        out_shape=(
            jax.ShapeDtypeStruct((rows_n, width), BF16),
            jax.ShapeDtypeStruct((rows_n, width), F32),
            jax.ShapeDtypeStruct((2 * BLK, width), BF16),
            jax.ShapeDtypeStruct((peers_n // 2 * rows_n, width), BF16),
            jax.ShapeDtypeStruct((peers_n // 2 * rows_n, width), BF16),
            jax.ShapeDtypeStruct((rows_n, width), BF16),
            jax.ShapeDtypeStruct((rows_n, width), BF16),
        ),
        in_specs=[smem] + [hbm] * 10,
        out_specs=(vmem,) * 7,
        scratch_shapes=[
            pltpu.VMEM(tiles.shape, BF16),
            pltpu.VMEM(degree.shape, degree.dtype),
            pltpu.VMEM(w_self.shape, BF16),
            pltpu.VMEM(w_nbr.shape, BF16),
            pltpu.VMEM(bias.shape, F32),
            pltpu.VMEM(cot.shape, BF16),
            pltpu.VMEM(((table_n + 1) * BLK, width), BF16),
            pltpu.VMEM(((owners_n + 1) * BLK, width), F32),
            pltpu.SemaphoreType.DMA((6,)),
            pltpu.SemaphoreType.DMA((blocks_n,)),
            pltpu.SemaphoreType.DMA((2 + recv.size,)),
        ],
        compiler_params=pltpu.CompilerParams(vmem_limit_bytes=56 * 2**20),
        cost_estimate=pl.CostEstimate(
            flops=1_300_000_000, bytes_accessed=12_000_000, transcendentals=rows_n * width
        ),
        name="layer",
    )(plan, gathered, below, above, rows, tiles, degree, w_self, w_nbr, bias, cot)


def weights_kernel(rows_ref, mean_ref, pre_grad_ref, out_ref):
    width = rows_ref.shape[1]
    pre_grad = pre_grad_ref[...]
    bias_sum = jnp.sum(pre_grad.astype(F32), axis=0, keepdims=True)
    grads = [dot(rows_ref[...], pre_grad, ROWS_T), dot(mean_ref[...], pre_grad, ROWS_T)]
    grad_all = jnp.concatenate(grads, axis=0).astype(BF16)
    parts, each = out_ref.shape[0], out_ref.shape[1] - PAD
    halves = width // BLK
    lines = [bias_sum[:, i * BLK : (i + 1) * BLK] for i in range(halves)]
    lines.append(jnp.zeros((PAD - halves, BLK), F32))
    bias_tile = jnp.concatenate(lines, axis=0).astype(BF16)
    stride = parts // halves
    for i in range(halves):
        chunk = grad_all[:, i * BLK : (i + 1) * BLK].reshape(stride, each, BLK)
        out_ref[pl.ds(i * stride, stride), pl.ds(0, each), :] = chunk
    out_ref[:, pl.ds(each, PAD), :] = jnp.broadcast_to(bias_tile[None], (parts, PAD, BLK))


def weights(rows, mean_rows, pre_grad, parts):
    rows_n, width = rows.shape
    each = 2 * width * (width // BLK) // parts
    vmem = pl.BlockSpec(memory_space=pltpu.VMEM)
    return pl.pallas_call(
        weights_kernel,
        out_shape=jax.ShapeDtypeStruct((parts, each + PAD, BLK), BF16),
        in_specs=[vmem] * 3,
        out_specs=vmem,
        compiler_params=pltpu.CompilerParams(vmem_limit_bytes=16 * 2**20),
        cost_estimate=pl.CostEstimate(
            flops=4 * rows_n * width * width, bytes_accessed=1_200_000, transcendentals=0
        ),
        name="weights",
    )(rows, mean_rows, pre_grad)


def shift(block_rows, axis, step):
    count = math.prod(lax.axis_size(name) for name in axis)
    pairs = [(i, i + step) for i in range(count) if 0 <= i + step < count]
    return lax.ppermute(block_rows, axis, pairs)


def swap(array, axis):
    return lax.all_to_all(array, axis, split_axis=0, concat_axis=0, tiled=True)


def on_device(
    features, send_list, nbr_count, nbr_index, tiles, degree, w_self, w_nbr, bias, cotangent
):
    rows = features[0]
    rows_n, width = rows.shape
    blocks_n = rows_n // BLK
    links_n = nbr_index.shape[-1]
    groups = lax.axis_size("hi") * lax.axis_size("lo")
    doms = lax.axis_size("dom")

    with jax.named_scope("gather_rows"):
        lists = jnp.pad(send_list.reshape(1, -1).astype(BF16), ((0, PAD - 1), (0, width - send_list.size)))
        wide = jnp.concatenate([rows, lists], axis=0).astype(F32) * SCALE
        packed = lax.all_gather(wide.astype(jnp.float16), "dom", tiled=True)
        gathered = (packed.astype(F32) * (1.0 / SCALE)).astype(BF16)
        lists = packed.reshape(doms, rows_n + PAD, width)[:, rows_n]
        slots = send_list.shape[-1]
        recv = lax.dynamic_slice_in_dim(lists, lax.axis_index("dom") * slots, slots, axis=1)
        recv = jnp.round(recv.astype(F32) * (1.0 / SCALE)).astype(jnp.int32)
    with jax.named_scope("rims"):
        below = shift(rows[rows_n - BLK :], GRP, 1)
        above = shift(rows[:BLK], GRP, -1)

    hidden, base, rims, keep, give, mean_rows, pre_grad = layer(
        recv,
        nbr_count[0, 0],
        nbr_index[0, 0],
        lax.axis_index("dom") % 2,
        gathered,
        below,
        above,
        rows,
        tiles.reshape(blocks_n * links_n, BLK, BLK),
        degree.reshape(blocks_n, BLK),
        w_self,
        w_nbr,
        bias.reshape(1, width),
        cotangent[0],
    )

    with jax.named_scope("return_slots"):
        taken = lax.ppermute(give, "dom", [(i, i ^ 1) for i in range(doms)])
        partial = weights(rows, mean_rows, pre_grad, lax.axis_size("lo"))
        taken, partial = lax.optimization_barrier((taken, partial))
        merged = (keep.astype(F32) + taken.astype(F32)).astype(BF16)
        rings = [list(range(core, doms, 2)) for core in range(2)]
        returned = lax.psum_scatter(merged, "dom", tiled=True, axis_index_groups=rings)
    with jax.named_scope("return_rims"):
        from_above = shift(rims[:BLK], GRP, -1)
        from_below = shift(rims[BLK:], GRP, 1)
    with jax.named_scope("weight_sums"):
        chunk = jnp.sum(swap(partial, "lo").astype(F32), axis=0)
        chunk = jnp.sum(lax.all_gather(chunk, ("dom", "hi")), axis=0)
        chunk = chunk * (1.0 / math.sqrt(rows_n * doms * groups))
        halves = width // BLK
        each = chunk.shape[0] - PAD
        bias_grad = chunk[each : each + halves].reshape(width)
        finished = chunk[:each].astype(BF16)
        whole = swap(jnp.broadcast_to(finished[None], (lax.axis_size("lo"), each, BLK)), "lo")
        whole = whole.reshape(halves, 2 * width, BLK).astype(F32)
        whole = jnp.concatenate([whole[i] for i in range(halves)], axis=1)
    edges = jnp.concatenate(
        [from_below, jnp.zeros((rows_n - 2 * BLK, width), BF16), from_above], axis=0
    )
    feat_grad = base + returned.astype(F32) + edges.astype(F32)
    return hidden[None], feat_grad[None], whole[:width], whole[width:], bias_grad


def solution(mesh):
    doms, groups = mesh.devices.shape
    split = Mesh(mesh.devices.reshape(doms, 2, groups // 2), ("dom",) + GRP)
    in_specs = (
        P("dom", GRP, None),
        P("dom", GRP, None, None),
        P("dom", GRP, None),
        P("dom", GRP, None, None),
        P("dom", GRP, None, None, None),
        P("dom", GRP),
        P(),
        P(),
        P(),
        P("dom", GRP, None),
    )
    out_specs = (P("dom", GRP, None), P("dom", GRP, None), P(), P(), P())
    return jax.shard_map(
        on_device, mesh=split, in_specs=in_specs, out_specs=out_specs, check_vma=False
    )
```

```python
import functools
import math

import jax
import jax.numpy as jnp
from jax import lax
from jax.experimental import pallas as pl
from jax.experimental.pallas import tpu as pltpu
from jax.sharding import PartitionSpec as P

BLK = 128
PAD = 16
SCALE = 8192.0
F32 = jnp.float32
BF16 = jnp.bfloat16
ROWS_T = (((0,), (0,)), ((), ()))
COLS_T = (((1,), (1,)), ((), ()))


def dot(a, b, dims=(((1,), (0,)), ((), ()))):
    return lax.dot_general(a, b, dims, preferred_element_type=F32)


def block(t):
    return pl.ds(pl.multiple_of(t * BLK, BLK), BLK)


def layer_kernel(
    blocks_n,
    links_n,
    peers_n,
    per_peer,
    plan_ref,
    gathered_ref,
    below_ref,
    above_ref,
    rows_hbm,
    tiles_hbm,
    degree_hbm,
    w_self_hbm,
    w_nbr_hbm,
    bias_hbm,
    cot_hbm,
    hidden_hbm,
    base_hbm,
    rims_hbm,
    sends_hbm,
    weights_hbm,
    hidden_ref,
    base_ref,
    rims_ref,
    sends_ref,
    weights_ref,
    tiles_ref,
    degree_ref,
    w_self_ref,
    w_nbr_ref,
    bias_ref,
    cot_ref,
    table,
    grads,
    own_sems,
    tile_sems,
    table_sems,
    out_sems,
    send_sems,
):
    rows_n, width = cot_ref.shape
    halo = blocks_n + 2
    slots_n = peers_n * per_peer
    table_n = halo + slots_n
    rows_ref = table.at[pl.ds(0, rows_n)]
    own = [
        pltpu.make_async_copy(source, target, own_sems.at[i])
        for i, (source, target) in enumerate(
            (
                (rows_hbm, rows_ref),
                (w_self_hbm, w_self_ref),
                (degree_hbm, degree_ref),
                (bias_hbm, bias_ref),
                (w_nbr_hbm, w_nbr_ref),
                (cot_hbm, cot_ref),
            )
        )
    ]
    tile_copies = [
        pltpu.make_async_copy(
            tiles_hbm.at[pl.ds(b * links_n, links_n)],
            tiles_ref.at[pl.ds(b * links_n, links_n)],
            tile_sems.at[b],
        )
        for b in range(blocks_n)
    ]
    table_copies = [
        pltpu.make_async_copy(below_ref, table.at[pl.ds(blocks_n * BLK, BLK)], table_sems.at[0]),
        pltpu.make_async_copy(above_ref, table.at[pl.ds((blocks_n + 1) * BLK, BLK)], table_sems.at[1]),
    ]
    for slot in range(slots_n):
        source = (slot // per_peer) * (rows_n + PAD) + jnp.maximum(plan_ref[slot], 0) * BLK
        table_copies.append(
            pltpu.make_async_copy(
                gathered_ref.at[pl.ds(pl.multiple_of(source, PAD), BLK)],
                table.at[pl.ds((halo + slot) * BLK, BLK)],
                table_sems.at[2 + slot],
            )
        )
    for copy in own + table_copies + tile_copies:
        copy.start()
    outs = []

    def write_out(source, target, sem):
        outs.append(pltpu.make_async_copy(source, target, sem))
        outs[-1].start()

    table[pl.ds(table_n * BLK, BLK)] = jnp.zeros((BLK, width), BF16)
    grads[...] = jnp.zeros_like(grads)
    entries = []
    owners = []
    for b in range(blocks_n):
        count = plan_ref[slots_n + b]
        for k in range(links_n):
            entry = plan_ref[slots_n + blocks_n + b * links_n + k]
            is_slot = entry >= halo
            slot = jnp.maximum(entry - halo, 0)
            owner = plan_ref[slot]
            dead = (k >= count) | (is_slot & (owner < 0))
            entries.append(jnp.where(dead, table_n, entry))
            owner = jnp.where(is_slot, halo + (slot // per_peer) * blocks_n + owner, entry)
            owners.append(jnp.where(dead, halo + peers_n * blocks_n, owner))

    for copy in own:
        copy.wait()
    rows = rows_ref[...]
    self_act = dot(rows, w_self_ref[...]) + bias_ref[...]
    spreads = []
    for b in range(blocks_n):
        line = degree_ref[pl.ds(b, 1), :].astype(F32)
        column = jnp.transpose(jnp.broadcast_to(line, (BLK, BLK)))
        spreads.append(jnp.concatenate([column] * (width // BLK), axis=1))
    for copy in table_copies:
        copy.wait()

    means = []
    for b in range(blocks_n):
        tile_copies[b].wait()
        total = None
        for k in range(0, links_n, 2):
            at = b * links_n + k
            left = jnp.concatenate([tiles_ref[at], tiles_ref[at + 1]], axis=1)
            right = jnp.concatenate([table[block(entries[at])], table[block(entries[at + 1])]], axis=0)
            term = dot(left, right)
            total = term if total is None else total + term
        means.append((total / spreads[b]).astype(BF16))
    mean_rows = jnp.concatenate(means, axis=0)
    pre_act = self_act + dot(mean_rows, w_nbr_ref[...])
    gate = jax.nn.sigmoid(pre_act)
    hidden_ref[...] = (pre_act * gate).astype(BF16)
    write_out(hidden_ref, hidden_hbm, out_sems.at[0])
    slope = gate * (1.0 + pre_act * (1.0 - gate))
    pre_grad = (cot_ref[...].astype(F32) * slope).astype(BF16)
    grad_all = jnp.concatenate([dot(rows, pre_grad, ROWS_T), dot(mean_rows, pre_grad, ROWS_T)], axis=0)
    grad_all = grad_all.astype(BF16)
    bias_sum = jnp.sum(pre_grad.astype(F32), axis=0, keepdims=True)
    parts, each = weights_ref.shape[0], weights_ref.shape[1] // 2
    halves = width // BLK
    lines = [bias_sum[:, i * BLK : (i + 1) * BLK] for i in range(halves)]
    lines.append(jnp.zeros((each - halves, BLK), F32))
    bias_tile = jnp.concatenate(lines, axis=0).astype(BF16)
    stride = parts // halves
    for i in range(halves):
        chunk = grad_all[:, i * BLK : (i + 1) * BLK].reshape(stride, each, BLK)
        weights_ref[pl.ds(i * stride, stride), pl.ds(0, each), :] = chunk
    weights_ref[:, pl.ds(each, each), :] = jnp.broadcast_to(bias_tile[None], (parts, each, BLK))
    write_out(weights_ref, weights_hbm, out_sems.at[1])

    mean_grad = dot(pre_grad, w_nbr_ref[...], COLS_T)
    for b in range(blocks_n):
        sum_grad = (mean_grad[b * BLK : (b + 1) * BLK] / spreads[b]).astype(BF16)
        side_by_side = jnp.concatenate([tiles_ref[b * links_n + k] for k in range(links_n)], axis=1)
        products = dot(side_by_side, sum_grad, ROWS_T)
        for k in range(links_n):
            grads[block(owners[b * links_n + k])] += products[k * BLK : (k + 1) * BLK]
    for p in range(peers_n):
        here = pl.ds(p * rows_n, rows_n)
        sends_ref[here] = grads[pl.ds(halo * BLK + p * rows_n, rows_n)].astype(BF16)
        write_out(sends_ref.at[here], sends_hbm.at[here], send_sems.at[p])
    rims_ref[...] = grads[pl.ds(rows_n, 2 * BLK)].astype(BF16)
    write_out(rims_ref, rims_hbm, out_sems.at[2])
    base_ref[...] = dot(pre_grad, w_self_ref[...], COLS_T) + grads[pl.ds(0, rows_n)]
    write_out(base_ref, base_hbm, out_sems.at[3])
    for copy in outs:
        copy.wait()


def layer(recv, count, index, gathered, below, above, rows, tiles, degree, w_self, w_nbr, bias, cot, parts):
    blocks_n, links_n = index.shape
    peers_n, per_peer = recv.shape
    rows_n, width = rows.shape
    table_n = blocks_n + 2 + recv.size
    owners_n = blocks_n + 2 + peers_n * blocks_n
    plan = jnp.concatenate([recv.reshape(-1), count, index.reshape(-1)])
    smem = pl.BlockSpec(memory_space=pltpu.SMEM)
    hbm = pl.BlockSpec(memory_space=pl.ANY)
    each = 2 * width * (width // BLK) // parts
    outs = (
        jax.ShapeDtypeStruct((rows_n, width), BF16),
        jax.ShapeDtypeStruct((rows_n, width), F32),
        jax.ShapeDtypeStruct((2 * BLK, width), BF16),
        jax.ShapeDtypeStruct((peers_n * rows_n, width), BF16),
        jax.ShapeDtypeStruct((parts, 2 * each, BLK), BF16),
    )
    return pl.pallas_call(
        functools.partial(layer_kernel, blocks_n, links_n, peers_n, per_peer),
        out_shape=outs,
        in_specs=[smem] + [hbm] * 10,
        out_specs=(hbm,) * 5,
        scratch_shapes=[pltpu.VMEM(out.shape, out.dtype) for out in outs]
        + [
            pltpu.VMEM(tiles.shape, BF16),
            pltpu.VMEM(degree.shape, degree.dtype),
            pltpu.VMEM(w_self.shape, BF16),
            pltpu.VMEM(w_nbr.shape, BF16),
            pltpu.VMEM(bias.shape, F32),
            pltpu.VMEM(cot.shape, BF16),
            pltpu.VMEM(((table_n + 1) * BLK, width), BF16),
            pltpu.VMEM(((owners_n + 1) * BLK, width), F32),
            pltpu.SemaphoreType.DMA((6,)),
            pltpu.SemaphoreType.DMA((blocks_n,)),
            pltpu.SemaphoreType.DMA((2 + recv.size,)),
            pltpu.SemaphoreType.DMA((4,)),
            pltpu.SemaphoreType.DMA((peers_n,)),
        ],
        compiler_params=pltpu.CompilerParams(vmem_limit_bytes=56 * 2**20),
        cost_estimate=pl.CostEstimate(
            flops=1_300_000_000, bytes_accessed=12_000_000, transcendentals=rows_n * width
        ),
        name="layer",
    )(plan, gathered, below, above, rows, tiles, degree, w_self, w_nbr, bias, cot)


def shift(block_rows, axis, step):
    count = lax.axis_size(axis)
    pairs = [(i, i + step) for i in range(count) if 0 <= i + step < count]
    return lax.ppermute(block_rows, axis, pairs)


def swap(array, axis):
    return lax.all_to_all(array, axis, split_axis=0, concat_axis=0, tiled=True)


def on_device(
    features, send_list, nbr_count, nbr_index, tiles, degree, w_self, w_nbr, bias, cotangent
):
    rows = features[0]
    rows_n, width = rows.shape
    blocks_n = rows_n // BLK
    links_n = nbr_index.shape[-1]
    groups = lax.axis_size("grp")
    doms = lax.axis_size("dom")

    with jax.named_scope("gather_rows"):
        lists = jnp.pad(send_list.reshape(1, -1).astype(BF16), ((0, PAD - 1), (0, width - send_list.size)))
        wide = jnp.concatenate([rows, lists], axis=0).astype(F32) * SCALE
        packed = lax.all_gather(wide.astype(jnp.float16), "dom", tiled=True)
        below = shift(rows[rows_n - BLK :], "grp", 1)
        above = shift(rows[:BLK], "grp", -1)
        packed, below, above = lax.optimization_barrier((packed, below, above))
        gathered = (packed.astype(F32) * (1.0 / SCALE)).astype(BF16)
        lists = packed.reshape(doms, rows_n + PAD, width)[:, rows_n]
        slots = send_list.shape[-1]
        recv = lax.dynamic_slice_in_dim(lists, lax.axis_index("dom") * slots, slots, axis=1)
        recv = jnp.round(recv.astype(F32) * (1.0 / SCALE)).astype(jnp.int32)
    hidden, base, rims, sends, partial = layer(
        recv,
        nbr_count[0, 0],
        nbr_index[0, 0],
        gathered,
        below,
        above,
        rows,
        tiles.reshape(blocks_n * links_n, BLK, BLK),
        degree.reshape(blocks_n, BLK),
        w_self,
        w_nbr,
        bias.reshape(1, width),
        cotangent[0],
        groups,
    )

    with jax.named_scope("return_slots"):
        returned = lax.psum_scatter(sends, "dom", tiled=True)
    with jax.named_scope("return_rims"):
        from_above = shift(rims[:BLK], "grp", -1)
        from_below = shift(rims[BLK:], "grp", 1)
    with jax.named_scope("weight_sums"):
        chunk = jnp.sum(swap(partial, "grp").astype(F32), axis=0)
        chunk = jnp.sum(lax.all_gather(chunk, "dom"), axis=0)
        chunk = chunk * (1.0 / math.sqrt(rows_n * doms * groups))
        halves = width // BLK
        each = chunk.shape[0] // 2
        bias_grad = chunk[each : each + halves].reshape(width)
        finished = chunk[:each].astype(BF16)
        whole = swap(jnp.broadcast_to(finished[None], (groups, each, BLK)), "grp")
        whole = whole.reshape(halves, 2 * width, BLK).astype(F32)
        whole = jnp.concatenate([whole[i] for i in range(halves)], axis=1)
    edges = jnp.concatenate(
        [from_below, jnp.zeros((rows_n - 2 * BLK, width), BF16), from_above], axis=0
    )
    feat_grad = base + returned.astype(F32) + edges.astype(F32)
    return hidden[None], feat_grad[None], whole[:width], whole[width:], bias_grad


def solution(mesh):
    in_specs = (
        P("dom", "grp", None),
        P("dom", "grp", None, None),
        P("dom", "grp", None),
        P("dom", "grp", None, None),
        P("dom", "grp", None, None, None),
        P("dom", "grp"),
        P(),
        P(),
        P(),
        P("dom", "grp", None),
    )
    out_specs = (P("dom", "grp", None), P("dom", "grp", None), P(), P(), P())
    return jax.shard_map(
        on_device, mesh=mesh, in_specs=in_specs, out_specs=out_specs, check_vma=False
    )
```
